256 devices in a mesh: dp: 8 (over y, core), seq: 32 (over x, z).
Axes of the slice: x: 4, y: 4, z: 8, core: 2. Of those that a mesh axis runs over, the one named last changes fastest.
Arguments:
- states: bfloat16 [8, 8192, 5120], P('dp', 'seq'), may hold values from -6 to 6
- span_start: int32 [8, 512], P('dp', 'seq'), may hold values from 0 to 8191, as said below
- span_end: int32 [8, 512], P('dp', 'seq'), may hold values from 0 to 8191, as said below
- gold: int32 [8, 512], P('dp', 'seq'), may hold values from 0 to 47
- live: int32 [8, 512], P('dp', 'seq'), may hold values 0 or 1
- start_proj: bfloat16 [5120, 1024], P('seq'), may hold values from -0.078125 to 0.078125
- end_proj: bfloat16 [5120, 1024], P('seq'), may hold values from -0.078125 to 0.078125
- biaffine: bfloat16 [48, 1024, 1024], P(None, 'seq'), may hold values from -64 to 64
Outputs:
- span_loss: float32 [8, 512], P('dp', 'seq')
- grad_start: bfloat16 [5120, 1024], P('seq')
- grad_end: bfloat16 [5120, 1024], P('seq')
- grad_biaffine: bfloat16 [48, 1024, 1024], P(None, 'seq')
The draws below stay inside these ranges and needn't reach their ends.
Inputs may be any that keep to these rules, and one draw needn't show every extreme that they name: `span_start`: the tokens of a schema form 2 * 32 blocks of 128 tokens; index j of seq holds block j and then the mirrored block from the far end. Span s has its start and its end in one of the two blocks held by index s // 16 of seq. span_start <= span_end <= span_start + 31, both in the same block.
All inputs are finite; a program needn't handle non-finite values. No bound on the sum of `live` on one device may be relied on, other than what follows from the above.
Results may differ from the reference program's by a relative error of at most 0.012.
Values may be sent and summed in bfloat16 or wider, within the bound.
No kernel may reach another device: no remote copies, remote signals or barrier semaphores. Data moves between devices by JAX's collectives and lax.ppermute only.
A program may use at most 64 MiB of HBM per device.

```python
import jax
import jax.numpy as jnp
from jax import lax

D = 5120
R = 1024
L = 48
MAXW = 32
TOK_DEV = 256
SPAN_DEV = 16
BATCH = 8
TOKENS = 8192
SPANS = 512


def span_pair(key):
    shard_count = TOKENS // TOK_DEV
    half_rows = TOK_DEV // 2
    side_key, width_key, offset_key = jax.random.split(key, 3)
    owner_idx = jnp.arange(SPANS, dtype=jnp.int32) // SPAN_DEV
    owner_idx = jnp.broadcast_to(owner_idx[None, :], (BATCH, SPANS))
    side_bit = jax.random.randint(side_key, (BATCH, SPANS), 0, 2)
    block_idx = jnp.where(side_bit == 1, 2 * shard_count - 1 - owner_idx, owner_idx)
    extent = jax.random.randint(width_key, (BATCH, SPANS), 0, MAXW)
    offset = jax.random.randint(offset_key, (BATCH, SPANS), 0, half_rows - extent)
    first_tok = block_idx * half_rows + offset
    return (first_tok.astype(jnp.int32), (first_tok + extent).astype(jnp.int32))


def draw_span_start(key, part):
    first_tok, last_tok = span_pair(key)
    return first_tok


def draw_span_end(key, part):
    first_tok, last_tok = span_pair(key)
    return last_tok


def draw_biaffine(key, part):
    key = jax.random.fold_in(key, 7)
    base_key = jax.random.fold_in(key, 0)
    spread_scale = 7.0 / R
    base_draw = spread_scale * jnp.clip(jax.random.normal(base_key, (L, R, R), jnp.float32), -4.0, 4.0)
    return base_draw.astype(jnp.bfloat16)


def touch_ends(values, key, low, high):
    spot = [jax.random.randint(jax.random.fold_in(key, axis), (), 0, length) for axis, length in enumerate(values.shape)]
    main_axis = values.shape.index(max(values.shape))
    next_to = spot[:main_axis] + [(spot[main_axis] + 1) % values.shape[main_axis]] + spot[main_axis + 1:]
    return values.at[tuple(spot)].set(low).at[tuple(next_to)].set(high)


def levels(key, dims, pieces, smallest, high):
    factor_of = 1.0
    for position, shards_of in pieces:
        steps = jax.random.uniform(jax.random.fold_in(jax.random.fold_in(key, 6), position), (shards_of,), jnp.float32, smallest / len(pieces), high / len(pieces))
        factor_of = factor_of * jnp.repeat(jnp.exp(steps), dims[position] // shards_of).reshape((-1,) + (1,) * (len(dims) - 1 - position))
    return factor_of


def noise(own_key, shape, deviation, most, cuts=(), kind=jnp.bfloat16):
    gain = levels(own_key, shape, cuts, -0.22, 0.18) if cuts else 1.0
    values = jax.random.normal(own_key, shape, jnp.float32) * deviation * gain
    return jnp.minimum(jnp.maximum(values, -most), most).astype(kind)


def setup_inputs(seed: int = 0) -> dict:
    keys = jax.random.split(jax.random.key(seed), 9)
    states = noise(keys[0], (BATCH, TOKENS, D), 1.0, 6.0, ((0, 8), (1, 32)))
    span_start = draw_span_start(jax.random.fold_in(keys[8], 71), 0)
    span_end = draw_span_end(jax.random.fold_in(keys[8], 71), 0)
    gold = touch_ends(jax.random.randint(keys[3], (BATCH, SPANS), 0, L), jax.random.fold_in(keys[3], 1), 0, L - 1).astype(jnp.int32)
    live = touch_ends((jax.random.randint(keys[4], (BATCH, SPANS), 0, 4) < 3).astype(jnp.int32), jax.random.fold_in(keys[4], 1), 0, 1)
    start_proj = noise(keys[5], (D, R), D ** -0.5, 0.078125, ((0, 32),))
    end_proj = noise(keys[6], (D, R), D ** -0.5, 0.078125, ((0, 32),))
    biaffine = draw_biaffine(jax.random.fold_in(keys[8], 71), 0)
    return dict(states=states, span_start=span_start, span_end=span_end, gold=gold, live=live, start_proj=start_proj, end_proj=end_proj, biaffine=biaffine)


def token_rows(tokens):
    half_rows = TOK_DEV // 2
    shard_count = TOKENS // TOK_DEV
    block_idx = tokens // half_rows
    low_side = block_idx < shard_count
    device_idx = jnp.where(low_side, block_idx, 2 * shard_count - 1 - block_idx)
    local_row = jnp.where(low_side, tokens - block_idx * half_rows, half_rows + tokens - block_idx * half_rows)
    return (device_idx * TOK_DEV + local_row).astype(jnp.int32)

def schema_terms(schema_rows, starts, stops, gold_ids, live_ids, start_proj, end_proj, biaffine):
    first_state = jnp.take(schema_rows, token_rows(starts), axis=0)
    last_state = jnp.take(schema_rows, token_rows(stops), axis=0)
    pre_left = jnp.dot(first_state, start_proj, preferred_element_type=jnp.float32)
    pre_right = jnp.dot(last_state, end_proj, preferred_element_type=jnp.float32)
    left_full, left_back = jax.vjp(jax.nn.gelu, pre_left)
    right_full, right_back = jax.vjp(jax.nn.gelu, pre_right)
    left_act = left_full.astype(jnp.bfloat16)
    right_act = right_full.astype(jnp.bfloat16)
    left_wide = left_act.astype(jnp.float32)

    def score_label(weight):
        label_image = jnp.dot(right_act, weight.T, preferred_element_type=jnp.float32)
        return lax.optimization_barrier(jnp.sum(label_image * left_wide, axis=1))
    scores = lax.map(score_label, biaffine).T
    log_total = jax.nn.logsumexp(scores, axis=1)
    onehot = (gold_ids[:, None] == jnp.arange(L, dtype=jnp.int32)[None, :]).astype(jnp.float32)
    picked = lax.optimization_barrier(jnp.sum(scores * onehot, axis=1))
    live_wide = live_ids.astype(jnp.float32)
    span_loss = live_wide * (log_total - picked)
    softmax = jnp.exp(scores - log_total[:, None])
    slope = (live_wide[:, None] * (softmax - onehot) / SPAN_DEV).astype(jnp.bfloat16)
    slope_wide = slope.astype(jnp.float32)

    def back_label(running, inputs):
        weight, column = inputs
        grad_left, grad_right = running
        label_image = jnp.dot(right_act, weight.T, preferred_element_type=jnp.float32)
        grad_left = grad_left + column[:, None] * label_image
        outer_rows = (column[:, None] * left_wide).astype(jnp.bfloat16)
        grad_weight = jnp.dot(outer_rows.T, right_act, preferred_element_type=jnp.float32)
        grad_right = grad_right + jnp.dot(outer_rows, weight, preferred_element_type=jnp.float32)
        return ((grad_left, grad_right), grad_weight)
    zero_grads = (jnp.zeros((SPANS, R), jnp.float32), jnp.zeros((SPANS, R), jnp.float32))
    (grad_left, grad_right), grad_biaffine = lax.scan(back_label, zero_grads, (biaffine, slope_wide.T))
    lowered_left = left_back(grad_left)[0].astype(jnp.bfloat16)
    lowered_right = right_back(grad_right)[0].astype(jnp.bfloat16)
    grad_start = jnp.dot(first_state.T, lowered_left, preferred_element_type=jnp.float32)
    grad_end = jnp.dot(last_state.T, lowered_right, preferred_element_type=jnp.float32)
    return (span_loss, grad_start, grad_end, grad_biaffine)

def reference(states, span_start, span_end, gold, live, start_proj, end_proj, biaffine):
    losses = []
    total_start = jnp.zeros((D, R), jnp.float32)
    total_end = jnp.zeros((D, R), jnp.float32)
    total_biaffine = jnp.zeros((L, R, R), jnp.float32)
    for schema in range(BATCH):
        span_loss, grad_start, grad_end, grad_biaffine = schema_terms(states[schema], span_start[schema], span_end[schema], gold[schema], live[schema], start_proj, end_proj, biaffine)
        losses.append(span_loss)
        total_start = total_start + grad_start
        total_end = total_end + grad_end
        total_biaffine = total_biaffine + grad_biaffine
    return (jnp.stack(losses, axis=0), total_start.astype(jnp.bfloat16), total_end.astype(jnp.bfloat16), total_biaffine.astype(jnp.bfloat16))
```

```python
import jax
import jax.numpy as jnp
from jax import lax
from jax.sharding import PartitionSpec as P


def exchange(parts):
    return lax.all_to_all(parts, "seq", split_axis=0, concat_axis=0, tiled=True)


def spread(values, count):
    return exchange(jnp.broadcast_to(values[None], (count,) + values.shape))


def shards(states, span_start, span_end, gold, live, start_proj, end_proj, biaffine):
    seq_index = lax.axis_index("seq")
    half_rows = states.shape[1] // 2
    own = span_start.shape[1]
    labels, inner, full = biaffine.shape
    count = full // inner
    depth = start_proj.shape[0]
    spans = own * count

    def local_rows(tokens):
        block_idx = tokens // half_rows
        return jnp.where(
            block_idx == seq_index,
            tokens - block_idx * half_rows,
            half_rows + tokens - block_idx * half_rows,
        )

    picks = jnp.concatenate([local_rows(span_start[0]), local_rows(span_end[0])])
    pick_mat = (picks[:, None] == jnp.arange(2 * half_rows)[None, :]).astype(jnp.bfloat16)
    rows = jnp.dot(pick_mat, states[0], preferred_element_type=jnp.float32).astype(jnp.bfloat16)
    chunks = rows.reshape(2 * own, count, depth).transpose(1, 0, 2)
    tags = jnp.stack([gold[0], live[0]], axis=1).astype(jnp.bfloat16)
    tags = jnp.concatenate([tags, jnp.zeros_like(tags)], axis=0)
    tags = jnp.broadcast_to(tags[None], (count, 2 * own, 2))
    payload = jnp.concatenate([chunks, tags], axis=2)
    payload = jnp.pad(payload, ((0, 0), (0, 0), (0, 256 - depth - 2)))
    got = exchange(payload)
    first = got[:, :own, :depth].reshape(spans, depth)
    last = got[:, own:, :depth].reshape(spans, depth)
    gold_all = got[:, :own, depth].reshape(1, spans).astype(jnp.float32)
    live_all = got[:, :own, depth + 1].reshape(1, spans).astype(jnp.float32)

    def project(weight, piece):
        return lax.dot_general(
            weight, piece, (((0,), (1,)), ((), ())), preferred_element_type=jnp.float32
        ).astype(jnp.bfloat16).reshape(count, inner, spans)

    part = jnp.concatenate([project(start_proj, first), project(end_proj, last)], axis=1)
    pre = jnp.sum(exchange(part).astype(jnp.float32), axis=0)
    act, act_back = jax.vjp(jax.nn.gelu, pre)
    act = act.astype(jnp.bfloat16)
    left = act[:inner].astype(jnp.float32)
    right = spread(act[inner:], count).reshape(full, spans)
    flat_weight = biaffine.reshape(labels * inner, full)
    image = jnp.dot(flat_weight, right, preferred_element_type=jnp.float32).reshape(
        labels, inner, spans
    )
    part_scores = jnp.sum(image * left[None], axis=1)
    score_parts = part_scores.reshape(labels, count, own).transpose(1, 0, 2)
    own_scores = jnp.sum(exchange(score_parts), axis=0)
    scores = spread(own_scores, count).transpose(1, 0, 2).reshape(labels, spans)
    log_total = jax.nn.logsumexp(scores, axis=0, keepdims=True)
    onehot = (gold_all == jnp.arange(labels, dtype=jnp.float32)[:, None]).astype(jnp.float32)
    picked = jnp.sum(scores * onehot, axis=0, keepdims=True)
    loss_all = live_all * (log_total - picked)
    span_loss = lax.dynamic_slice_in_dim(loss_all, seq_index * own, own, 1)
    slope = (live_all * (jnp.exp(scores - log_total) - onehot) / own).astype(jnp.bfloat16)
    slope_wide = slope.astype(jnp.float32)
    grad_left = jnp.sum(slope_wide[:, None, :] * image, axis=0)
    outer = (slope_wide[:, None, :] * left[None]).astype(jnp.bfloat16).reshape(labels * inner, spans)
    grad_right_part = lax.dot_general(
        flat_weight, outer, (((0,), (0,)), ((), ())), preferred_element_type=jnp.float32
    ).astype(jnp.bfloat16)
    grad_flat = lax.dot_general(
        outer, right, (((1,), (1,)), ((), ())), preferred_element_type=jnp.float32
    )
    sum_flat = lax.psum(grad_flat, "dp").astype(jnp.bfloat16)
    grad_right = jnp.sum(
        exchange(grad_right_part.reshape(count, inner, spans)).astype(jnp.float32), axis=0
    )
    lowered = act_back(jnp.concatenate([grad_left, grad_right], axis=0))[0].astype(jnp.bfloat16)
    lowered_all = spread(lowered, count)
    low_left = lowered_all[:, :inner].reshape(full, spans)
    low_right = lowered_all[:, inner:].reshape(full, spans)

    def weight_grad(piece, low):
        return lax.dot_general(
            piece, low, (((0,), (1,)), ((), ())), preferred_element_type=jnp.float32
        )

    grads = jnp.concatenate([weight_grad(first, low_left), weight_grad(last, low_right)], axis=0)
    batch = 8
    grad_parts = grads.astype(jnp.bfloat16).reshape(batch, 2 * depth // batch, full)
    grad_parts = lax.all_to_all(grad_parts, "dp", split_axis=0, concat_axis=0, tiled=True)
    grad_own = jnp.sum(grad_parts.astype(jnp.float32), axis=0).astype(jnp.bfloat16)
    grad_full = lax.all_to_all(
        jnp.broadcast_to(grad_own[None], (batch,) + grad_own.shape),
        "dp",
        split_axis=0,
        concat_axis=0,
        tiled=True,
    ).reshape(2 * depth, full)
    return (
        span_loss,
        grad_full[:depth],
        grad_full[depth:],
        sum_flat.reshape(labels, inner, full),
    )


def solution(mesh):
    placed = (
        P("dp", "seq", None),
        P("dp", "seq"),
        P("dp", "seq"),
        P("dp", "seq"),
        P("dp", "seq"),
        P("seq", None),
        P("seq", None),
        P(None, "seq", None),
    )
    return jax.shard_map(
        shards,
        mesh=mesh,
        in_specs=placed,
        out_specs=(P("dp", "seq"), P("seq", None), P("seq", None), P(None, "seq", None)),
        check_vma=False,
    )
```

```python
import jax
import jax.numpy as jnp
from jax import lax
from jax.experimental import pallas as pl
from jax.experimental.pallas import tpu as pltpu
from jax.sharding import Mesh
from jax.sharding import PartitionSpec as P

CORES = 2
COLUMNS = 4
BF16 = jnp.bfloat16
F32 = jnp.float32


def exchange(parts, axes):
    return lax.all_to_all(parts, axes, split_axis=0, concat_axis=0, tiled=True)


def call(body, outs, args, scratch=(), smem=(), flops=0):
    moved = sum(a.size * a.dtype.itemsize for a in args)
    moved += sum(o.size * jnp.dtype(o.dtype).itemsize for o in outs)
    specs = [
        pl.BlockSpec(memory_space=pltpu.SMEM if i in smem else pltpu.VMEM)
        for i in range(len(args))
    ]
    got = pl.pallas_call(
        body,
        out_shape=tuple(outs),
        in_specs=specs,
        out_specs=tuple(pl.BlockSpec(memory_space=pltpu.VMEM) for _ in outs),
        scratch_shapes=list(scratch),
        compiler_params=pltpu.CompilerParams(vmem_limit_bytes=48 * 1024 * 1024),
        cost_estimate=pl.CostEstimate(flops=flops, bytes_accessed=moved, transcendentals=0),
    )(*args)
    return got


def dot(a, b, da, db):
    return lax.dot_general(a, b, (((da,), (db,)), ((), ())), preferred_element_type=F32)


def pick_body(nx, nz, seq_ref, start_ref, end_ref, states_ref, out_ref):
    tokens, width = states_ref.shape
    half = tokens // 2
    depth = width // (nx * nz)
    own = start_ref.shape[1]
    states = states_ref[...]
    for side, ref in enumerate((start_ref, end_ref)):
        token = ref[...]
        inside = lax.rem(token, half)
        low = (token - inside) == seq_ref[0] * half
        picks = inside + jnp.where(low, 0, half)
        spot = lax.broadcasted_iota(jnp.int32, (tokens, own), 0)
        mask = jnp.where(spot == picks, 1.0, 0.0).astype(BF16)
        rows = dot(mask, states, 0, 0)
        for z in range(nz):
            cut = [rows[:, (x * nz + z) * depth : (x * nz + z + 1) * depth] for x in range(nx)]
            out_ref[side * nz + z] = jnp.concatenate(cut, axis=1).astype(BF16)


def project_body(nx, nz, inner, weight_ref, piece_ref, out_ref):
    full = weight_ref.shape[2]
    weight = weight_ref[...].reshape(-1, full)
    piece = piece_ref[...].reshape(-1, piece_ref.shape[2])
    pre = dot(weight, piece, 0, 1).astype(BF16)
    group = pre.shape[1] // CORES
    for c in range(CORES):
        for z in range(nz):
            for x in range(nx):
                at = (x * nz + z) * inner
                out_ref[c * nz + z, x * inner : (x + 1) * inner, :] = pre[
                    at : at + inner, c * group : (c + 1) * group
                ]


def act_body(nx, nz, inner, got_ref, tags_ref, pre_ref, left_ref, right_ref):
    def total(side):
        sums = got_ref[side * nz].astype(F32)
        for z in range(1, nz):
            sums = sums + got_ref[side * nz + z].astype(F32)
        return sums

    pre_left, pre_right = total(0), total(1)
    pre_ref[0] = pre_left
    pre_ref[1] = pre_right
    left = jax.nn.gelu(pre_left).astype(BF16)
    right = jax.nn.gelu(pre_right)
    tags = tags_ref[...]
    for x in range(nx):
        left_ref[x] = left
        block = jnp.concatenate([right[x * inner : (x + 1) * inner], tags], axis=0).astype(BF16)
        for z in range(nz):
            right_ref[x * nz + z] = block


def score_body(nx, nz, inner, weight_ref, left_got, right_got, out_ref, left_ref, right_ref):
    labels = weight_ref.shape[1]
    width = weight_ref.shape[3]
    group = left_got.shape[2]
    for x in range(nx):
        left_ref[:, x * group : (x + 1) * group] = left_got[x].astype(F32)
        for z in range(nz):
            block = right_got[x * nz + z]
            right_ref[z * inner : (z + 1) * inner, x * group : (x + 1) * group] = block[:inner]
    for i in range(nx * nz):
        if i % nz >= labels // 8:
            out_ref[i] = jnp.zeros((8, group), F32)

    def step(lb, carry):
        total = jnp.zeros((8, nx * group), F32)
        for x in range(nx):
            weight = weight_ref[x, pl.ds(lb * 8, 8)].reshape(8 * inner, width)
            image = dot(weight, right_ref[...], 1, 0).reshape(8, inner, nx * group)
            left = left_ref[x * inner : (x + 1) * inner, :]
            total = total + jnp.sum(image * left[None], axis=1)
        for x in range(nx):
            out_ref[x * nz + lb] = total[:, x * group : (x + 1) * group]
        return carry

    lax.fori_loop(0, labels // 8, step, 0)


def slope_body(
    nx, nz, inner, own, weight_ref, left_ref, right_ref, right_got, score_ref,
    left_out, right_out, slope_ref, loss_ref, left_sum, right_sum,
):
    labels = weight_ref.shape[1]
    width = weight_ref.shape[3]
    group = score_ref.shape[2]
    for x in range(nx):
        lanes = slice(x * group, (x + 1) * group)
        tags = right_got[x * nz].astype(F32)[inner:]
        for z in range(1, nz):
            tags = tags + right_got[x * nz + z].astype(F32)[inner:]
        gold, live = tags[0:1], tags[1:2]
        scores = jnp.concatenate([score_ref[x * nz + b] for b in range(labels // 8)], axis=0)
        most = jnp.max(scores, axis=0, keepdims=True)
        log_total = most + jnp.log(jnp.sum(jnp.exp(scores - most), axis=0, keepdims=True))
        spot = lax.broadcasted_iota(jnp.int32, scores.shape, 0).astype(F32)
        onehot = jnp.where(spot == gold, 1.0, 0.0)
        picked = jnp.sum(scores * onehot, axis=0, keepdims=True)
        loss_ref[:, lanes] = live * (log_total - picked)
        slope = live * (jnp.exp(scores - log_total) - onehot) / own
        slope_ref[:, lanes] = slope.astype(BF16).astype(F32)
    left_sum[...] = jnp.zeros_like(left_sum)
    right_sum[...] = jnp.zeros_like(right_sum)

    def step(lb, carry):
        slope = slope_ref[pl.ds(lb * 8, 8), :]
        for x in range(nx):
            rows = slice(x * inner, (x + 1) * inner)
            weight = weight_ref[x, pl.ds(lb * 8, 8)].reshape(8 * inner, width)
            image = dot(weight, right_ref[...], 1, 0).reshape(8, inner, nx * group)
            left_sum[rows, :] += jnp.sum(image * slope[:, None, :], axis=0)
            left = left_ref[rows, :]
            outer = (slope[:, None, :] * left[None]).astype(BF16).reshape(8 * inner, nx * group)
            right_sum[...] += dot(weight, outer, 0, 0)
        return carry

    lax.fori_loop(0, labels // 8, step, 0)
    for x in range(nx):
        lanes = slice(x * group, (x + 1) * group)
        left_out[x] = left_sum[:, lanes].astype(BF16)
        for z in range(nz):
            right_out[x * nz + z] = right_sum[z * inner : (z + 1) * inner, lanes].astype(BF16)


def flat_body(nx, inner, left_ref, right_ref, slope_ref, out_ref):
    parts, _, take = out_ref.shape[:3]
    spans = left_ref.shape[1]
    for g in range(parts):
        slope = slope_ref[g * take : (g + 1) * take, :]
        for x in range(nx):
            left = left_ref[x * inner : (x + 1) * inner, :]
            outer = (slope[:, None, :] * left[None]).astype(BF16).reshape(take * inner, spans)
            out_ref[g, x] = dot(outer, right_ref[...], 1, 1).astype(BF16).reshape(out_ref.shape[2:])


def lower_body(nx, nz, inner, pre_ref, left_got, right_got, out_ref):
    grad_left = left_got[0].astype(F32)
    for x in range(1, nx):
        grad_left = grad_left + left_got[x].astype(F32)
    blocks = []
    for x in range(nx):
        block = right_got[x * nz].astype(F32)
        for z in range(1, nz):
            block = block + right_got[x * nz + z].astype(F32)
        blocks.append(block)
    grad_right = jnp.concatenate(blocks, axis=0)
    for side, grad in enumerate((grad_left, grad_right)):
        _, back = jax.vjp(jax.nn.gelu, pre_ref[side])
        lowered = back(grad)[0].astype(BF16)
        for z in range(nz):
            out_ref[side * nz + z] = lowered


def weight_body(nx, nz, inner, low_ref, piece_ref, out_ref, wide_ref):
    group = low_ref.shape[2]
    for c in range(CORES):
        for z in range(nz):
            for x in range(nx):
                at = (x * nz + z) * inner
                wide_ref[at : at + inner, c * group : (c + 1) * group] = low_ref[
                    c * nz + z, x * inner : (x + 1) * inner, :
                ]
    piece = piece_ref[...].reshape(-1, piece_ref.shape[2])
    grad = dot(piece, wide_ref[...], 0, 1)
    take = out_ref.shape[1]
    ny = out_ref.shape[0] // nx
    for y in range(ny):
        for x in range(nx):
            at = (x * ny + y) * take
            out_ref[y * nx + x] = grad[at : at + take].astype(BF16)


def build(ny, nx, nz):
    def shards(states, span_start, span_end, gold, live, start_proj, end_proj, biaffine):
        x_index, z_index = lax.axis_index("x"), lax.axis_index("z")
        seq_index = x_index * nz + z_index
        core = lax.axis_index("core")
        own = span_start.shape[1]
        labels, inner, full = biaffine.shape
        depth = start_proj.shape[0]
        group = own * nz
        spans = group * nx
        width = full // nx
        rows = nx * inner
        take = labels // (CORES * ny)
        shape = jax.ShapeDtypeStruct

        blocks = exchange(
            biaffine.reshape(labels, inner, nx, width).transpose(2, 0, 1, 3), "x"
        )
        side_proj = jnp.where(core == 0, start_proj, end_proj)
        weights = exchange(jnp.broadcast_to(side_proj[None], (nx,) + side_proj.shape), "x")

        (picked,) = call(
            lambda *refs: pick_body(nx, nz, *refs),
            [shape((CORES * nz, own, nx * depth), BF16)],
            (seq_index.reshape(1), span_start, span_end, states[0]),
            smem=(0,),
        )
        pieces = exchange(picked, ("core", "z"))

        (pre_parts,) = call(
            lambda *refs: project_body(nx, nz, inner, *refs),
            [shape((CORES * nz, rows, group), BF16)],
            (weights, pieces),
            flops=2 * full * nx * depth * group * CORES,
        )
        pre_got = exchange(pre_parts, ("core", "z"))

        tags = jnp.concatenate([gold, live], axis=0).astype(F32)
        tags = lax.dynamic_update_slice(jnp.zeros((8, group), F32), tags, (0, z_index * own))
        pre, left_pay, right_pay = call(
            lambda *refs: act_body(nx, nz, inner, *refs),
            [
                shape((2, rows, group), F32),
                shape((nx, rows, group), BF16),
                shape((nx * nz, inner + 8, group), BF16),
            ],
            (pre_got, tags),
        )
        right_got = exchange(right_pay, ("x", "z"))
        left_got = exchange(left_pay, "x")

        score_parts, left, right = call(
            lambda *refs: score_body(nx, nz, inner, *refs),
            [
                shape((nx * nz, 8, group), F32),
                shape((rows, spans), F32),
                shape((width, spans), BF16),
            ],
            (blocks, left_got, right_got),
            flops=2 * labels * rows * width * spans,
        )
        score_got = exchange(score_parts, ("x", "z"))
        score_sum = jnp.sum(score_got, axis=0)
        scores = exchange(jnp.broadcast_to(score_sum[None], score_got.shape), ("x", "z"))

        left_grad, right_grad, slope, loss = call(
            lambda *refs: slope_body(nx, nz, inner, own, *refs),
            [
                shape((nx, rows, group), BF16),
                shape((nx * nz, inner, group), BF16),
                shape((labels, spans), F32),
                shape((1, spans), F32),
            ],
            (blocks, left, right, right_got, scores),
            scratch=(pltpu.VMEM((rows, spans), F32), pltpu.VMEM((width, spans), F32)),
            flops=4 * labels * rows * width * spans,
        )
        span_loss = lax.dynamic_slice_in_dim(loss, seq_index * own, own, 1)
        right_grad_got = exchange(right_grad, ("x", "z"))
        left_grad_got = exchange(left_grad, "x")

        (flat,) = call(
            lambda *refs: flat_body(nx, inner, *refs),
            [shape((CORES * ny, nx, take, inner, width), BF16)],
            (left, right, slope),
            flops=2 * labels * rows * width * spans,
        )
        flat = exchange(flat.reshape((CORES, ny * nx) + flat.shape[2:]), "core")
        flat = jnp.sum(flat.astype(F32), axis=0).astype(BF16)
        flat = exchange(flat, "y").reshape((ny, nx) + flat.shape[1:])
        flat = jnp.sum(flat.astype(F32), axis=0).astype(BF16)
        flat = exchange(
            jnp.broadcast_to(flat[None], (ny,) + flat.shape).reshape((ny * nx,) + flat.shape[1:]),
            ("y", "x"),
        )
        flat = exchange(jnp.broadcast_to(flat[None], (CORES,) + flat.shape), "core")
        flat = flat.reshape(CORES * ny, nx, take, inner, width).transpose(0, 2, 3, 1, 4)
        grad_biaffine = flat.reshape(labels, inner, full)

        (lowered,) = call(
            lambda *refs: lower_body(nx, nz, inner, *refs),
            [shape((CORES * nz, rows, group), BF16)],
            (pre, left_grad_got, right_grad_got),
        )
        lowered_got = exchange(lowered, ("core", "z"))
        (grad_parts,) = call(
            lambda *refs: weight_body(nx, nz, inner, *refs),
            [shape((ny * nx, depth // ny, full), BF16)],
            (lowered_got, pieces),
            scratch=(pltpu.VMEM((full, CORES * group), BF16),),
            flops=2 * full * nx * depth * group * CORES,
        )
        grad_got = exchange(grad_parts, ("y", "x"))
        grad_own = jnp.sum(grad_got.astype(F32), axis=0).astype(BF16)
        grads = exchange(
            jnp.broadcast_to(grad_own[None], (ny * CORES,) + grad_own.shape), ("y", "core")
        ).reshape(ny, CORES, depth // ny, full)
        return (
            span_loss,
            grads[:, 0].reshape(depth, full),
            grads[:, 1].reshape(depth, full),
            grad_biaffine,
        )

    return shards


def solution(mesh):
    ny, nz = mesh.shape["dp"] // CORES, mesh.shape["seq"] // COLUMNS
    fine = Mesh(mesh.devices.reshape(ny, CORES, COLUMNS, nz), ("y", "core", "x", "z"))
    dp, seq = ("y", "core"), ("x", "z")
    placed = (
        P(dp, seq, None),
        P(dp, seq),
        P(dp, seq),
        P(dp, seq),
        P(dp, seq),
        P(seq, None),
        P(seq, None),
        P(None, seq, None),
    )
    return jax.shard_map(
        build(ny, COLUMNS, nz),
        mesh=fine,
        in_specs=placed,
        out_specs=(P(dp, seq), P(seq, None), P(seq, None), P(None, seq, None)),
        check_vma=False,
    )
```

```python
import jax
import jax.numpy as jnp
from jax import lax
from jax.experimental import pallas as pl
from jax.experimental.pallas import tpu as pltpu
from jax.sharding import Mesh
from jax.sharding import PartitionSpec as P

CORES = 2
COLUMNS = 4
TAGS = 16
BF16 = jnp.bfloat16
F32 = jnp.float32


def exchange(parts, axes):
    return lax.all_to_all(parts, axes, split_axis=0, concat_axis=0, tiled=True)


def call(body, outs, args, scratch=(), smem=(), flops=0):
    moved = sum(a.size * a.dtype.itemsize for a in args)
    moved += sum(o.size * jnp.dtype(o.dtype).itemsize for o in outs)
    specs = [
        pl.BlockSpec(memory_space=pltpu.SMEM if i in smem else pltpu.VMEM)
        for i in range(len(args))
    ]
    got = pl.pallas_call(
        body,
        out_shape=tuple(outs),
        in_specs=specs,
        out_specs=tuple(pl.BlockSpec(memory_space=pltpu.VMEM) for _ in outs),
        scratch_shapes=list(scratch),
        compiler_params=pltpu.CompilerParams(vmem_limit_bytes=48 * 1024 * 1024),
        cost_estimate=pl.CostEstimate(flops=flops, bytes_accessed=moved, transcendentals=0),
    )(*args)
    return got


def dot(a, b, da, db):
    return lax.dot_general(a, b, (((da,), (db,)), ((), ())), preferred_element_type=F32)


def pick_body(nx, nz, seq_ref, start_ref, end_ref, states_ref, out_ref):
    tokens, width = states_ref.shape
    half = tokens // 2
    depth = width // (nx * nz)
    own = start_ref.shape[1]
    states = states_ref[...]
    for side, ref in enumerate((start_ref, end_ref)):
        token = ref[...]
        inside = lax.rem(token, half)
        low = (token - inside) == seq_ref[0] * half
        picks = inside + jnp.where(low, 0, half)
        spot = lax.broadcasted_iota(jnp.int32, (tokens, own), 0)
        mask = jnp.where(spot == picks, 1.0, 0.0).astype(BF16)
        rows = dot(mask, states, 0, 0)
        for z in range(nz):
            cut = [rows[:, (x * nz + z) * depth : (x * nz + z + 1) * depth] for x in range(nx)]
            out_ref[side * nz + z] = jnp.concatenate(cut, axis=1).astype(BF16)


def project_body(nx, nz, inner, weight_ref, piece_ref, out_ref):
    full = weight_ref.shape[2]
    weight = weight_ref[...].reshape(-1, full)
    piece = piece_ref[...].reshape(-1, piece_ref.shape[2])
    pre = dot(weight, piece, 0, 1).astype(BF16)
    group = pre.shape[1] // CORES
    for c in range(CORES):
        for z in range(nz):
            for x in range(nx):
                at = (x * nz + z) * inner
                out_ref[c * nz + z, x * inner : (x + 1) * inner, :] = pre[
                    at : at + inner, c * group : (c + 1) * group
                ]


def act_body(nx, nz, got_ref, tags_ref, pre_ref, left_ref, right_ref):
    def total(side):
        sums = got_ref[side * nz].astype(F32)
        for z in range(1, nz):
            sums = sums + got_ref[side * nz + z].astype(F32)
        return sums

    pre_left, pre_right = total(0), total(1)
    pre_ref[0] = pre_left
    pre_ref[1] = pre_right
    left_ref[...] = jax.nn.gelu(pre_left).astype(BF16)
    block = jnp.concatenate([jax.nn.gelu(pre_right), tags_ref[...]], axis=0).astype(BF16)
    for z in range(nz):
        right_ref[z] = block


def spread_body(nx, nz, inner, left_ref, got_ref, out_ref):
    full = nx * nz * inner
    rows = nx * inner
    tags = got_ref[0].astype(F32)[rows:]
    for z in range(1, nz):
        tags = tags + got_ref[z].astype(F32)[rows:]
    tags = tags.astype(BF16)
    for to in range(nx):
        for z in range(nz):
            for x in range(nx):
                at = (x * nz + z) * inner
                out_ref[to, at : at + inner, :] = got_ref[z, x * inner : (x + 1) * inner, :]
        out_ref[to, full : full + inner, :] = left_ref[to * inner : (to + 1) * inner, :]
        out_ref[to, full + inner : full + inner + TAGS, :] = tags


def score_body(nx, nz, inner, weight_ref, got_ref, out_ref, left_ref, right_ref, tags_ref):
    labels, _, full = weight_ref.shape
    group = got_ref.shape[2]
    for x in range(nx):
        lanes = slice(x * group, (x + 1) * group)
        right_ref[:, lanes] = got_ref[x, :full, :]
        left_ref[:, lanes] = got_ref[x, full : full + inner, :].astype(F32)
        tags_ref[:, lanes] = got_ref[x, full + inner : full + inner + TAGS, :].astype(F32)
    for i in range(nx * nz):
        if i % nz >= labels // 8:
            out_ref[i] = jnp.zeros((8, group), F32)

    def step(lb, carry):
        weight = weight_ref[pl.ds(lb * 8, 8)].reshape(8 * inner, full)
        image = dot(weight, right_ref[...], 1, 0).reshape(8, inner, nx * group)
        total = jnp.sum(image * left_ref[...][None], axis=1)
        for x in range(nx):
            out_ref[x * nz + lb] = total[:, x * group : (x + 1) * group]
        return carry

    lax.fori_loop(0, labels // 8, step, 0)


def slope_body(
    nx, nz, inner, own, weight_ref, left_ref, right_ref, tags_ref, score_ref,
    out_ref, outer_ref, loss_ref, slope_ref,
):
    labels, _, full = weight_ref.shape
    group = score_ref.shape[2]
    spans = nx * group
    scores = jnp.concatenate(
        [
            jnp.concatenate([score_ref[x * nz + b] for x in range(nx)], axis=1)
            for b in range(labels // 8)
        ],
        axis=0,
    )
    gold, live = tags_ref[0:1, :], tags_ref[1:2, :]
    most = jnp.max(scores, axis=0, keepdims=True)
    log_total = most + jnp.log(jnp.sum(jnp.exp(scores - most), axis=0, keepdims=True))
    spot = lax.broadcasted_iota(jnp.int32, scores.shape, 0).astype(F32)
    onehot = jnp.where(spot == gold, 1.0, 0.0)
    picked = jnp.sum(scores * onehot, axis=0, keepdims=True)
    loss_ref[...] = live * (log_total - picked)
    slope = live * (jnp.exp(scores - log_total) - onehot) / own
    slope_ref[...] = slope.astype(BF16).astype(F32)

    def step(lb, left_sum):
        slope = slope_ref[pl.ds(lb * 8, 8), :]
        weight = weight_ref[pl.ds(lb * 8, 8)].reshape(8 * inner, full)
        image = dot(weight, right_ref[...], 1, 0).reshape(8, inner, spans)
        outer = (slope[:, None, :] * left_ref[...][None]).astype(BF16)
        outer_ref[pl.ds(lb * 8 * inner, 8 * inner), :] = outer.reshape(8 * inner, spans)
        return left_sum + jnp.sum(image * slope[:, None, :], axis=0)

    left_sum = lax.fori_loop(0, labels // 8, step, jnp.zeros((inner, spans), F32)).astype(BF16)
    weight = weight_ref[...].reshape(labels * inner, full)
    right_sum = dot(weight, outer_ref[...], 0, 0).astype(BF16)
    for to in range(nx):
        lanes = slice(to * group, (to + 1) * group)
        for z in range(nz):
            for x in range(nx):
                at = (x * nz + z) * inner
                spot = (z * nx + x) * inner
                out_ref[to, spot : spot + inner, :] = right_sum[at : at + inner, lanes]
        out_ref[to, full : full + inner, :] = left_sum[:, lanes]


def flat_body(outer_ref, right_ref, out_ref):
    out_ref[...] = dot(outer_ref[...], right_ref[...], 1, 1).astype(BF16)


def fold_body(nx, nz, got_ref, out_ref):
    _, rows, _ = out_ref.shape
    for z in range(nz):
        block = got_ref[0, z * rows : (z + 1) * rows, :].astype(F32)
        for x in range(1, nx):
            block = block + got_ref[x, z * rows : (z + 1) * rows, :].astype(F32)
        out_ref[z] = block.astype(BF16)


def lower_body(ny, nx, nz, inner, pre_ref, left_got, right_got, out_ref):
    full = nx * nz * inner
    grad_left = jnp.concatenate(
        [left_got[x, full : full + inner, :].astype(F32) for x in range(nx)], axis=0
    )
    grad_right = right_got[0].astype(F32)
    for z in range(1, nz):
        grad_right = grad_right + right_got[z].astype(F32)
    take = grad_left.shape[0] // ny
    for side, grad in enumerate((grad_left, grad_right)):
        _, back = jax.vjp(jax.nn.gelu, pre_ref[side])
        lowered = back(grad)[0].astype(BF16)
        for y in range(ny):
            for z in range(nz):
                out_ref[(y * CORES + side) * nz + z] = lowered[y * take : (y + 1) * take]


def weight_body(ny, nx, nz, inner, low_ref, piece_ref, out_ref, wide_ref):
    group = low_ref.shape[2]
    for s in range(ny * CORES):
        for z in range(nz):
            wide_ref[z * inner : (z + 1) * inner, s * group : (s + 1) * group] = low_ref[s * nz + z]
    piece = piece_ref[...].reshape(-1, piece_ref.shape[3])
    grad = dot(piece, wide_ref[...], 0, 1).astype(BF16)
    depth = out_ref.shape[1]
    for x in range(nx):
        out_ref[x] = grad[x * depth : (x + 1) * depth]


def total_body(got_ref, out_ref):
    total = got_ref[0].astype(F32)
    for x in range(1, got_ref.shape[0]):
        total = total + got_ref[x].astype(F32)
    total = total.astype(BF16)
    for i in range(out_ref.shape[0]):
        out_ref[i] = total


def join_body(got_ref, start_ref, end_ref):
    width = got_ref.shape[2]
    for y in range(got_ref.shape[0] // CORES):
        start_ref[:, y * width : (y + 1) * width] = got_ref[y * CORES]
        end_ref[:, y * width : (y + 1) * width] = got_ref[y * CORES + 1]


def build(ny, nx, nz):
    def shards(states, span_start, span_end, gold, live, start_proj, end_proj, biaffine):
        x_index, z_index = lax.axis_index("x"), lax.axis_index("z")
        seq_index = x_index * nz + z_index
        core = lax.axis_index("core")
        own = span_start.shape[1]
        labels, inner, full = biaffine.shape
        depth = start_proj.shape[0]
        group = own * nz
        spans = group * nx
        width = full // ny
        rows = nx * inner
        shape = jax.ShapeDtypeStruct

        side_proj = jnp.where(core == 0, start_proj, end_proj)
        weights = lax.all_gather(side_proj, "x", axis=0)

        (picked,) = call(
            lambda *refs: pick_body(nx, nz, *refs),
            [shape((CORES * nz, own, nx * depth), BF16)],
            (seq_index.reshape(1), span_start, span_end, states[0]),
            smem=(0,),
        )
        pieces = exchange(picked, ("core", "z"))
        all_pieces = lax.all_gather(pieces, "y", axis=0)

        (pre_parts,) = call(
            lambda *refs: project_body(nx, nz, inner, *refs),
            [shape((CORES * nz, rows, group), BF16)],
            (weights, pieces),
            flops=2 * full * nx * depth * group * CORES,
        )
        pre_got = exchange(pre_parts, ("core", "z"))

        tags = jnp.concatenate([gold, live], axis=0).astype(F32)
        tags = lax.dynamic_update_slice(jnp.zeros((TAGS, group), F32), tags, (0, z_index * own))
        pre, left_own, right_pay = call(
            lambda *refs: act_body(nx, nz, *refs),
            [
                shape((2, rows, group), F32),
                shape((rows, group), BF16),
                shape((nz, rows + TAGS, group), BF16),
            ],
            (pre_got, tags),
        )
        right_column = exchange(right_pay, "z")
        (act_pay,) = call(
            lambda *refs: spread_body(nx, nz, inner, *refs),
            [shape((nx, full + inner + TAGS, group), BF16)],
            (left_own, right_column),
        )
        act_got = exchange(act_pay, "x")

        score_parts, left, right, all_tags = call(
            lambda *refs: score_body(nx, nz, inner, *refs),
            [
                shape((nx * nz, 8, group), F32),
                shape((inner, spans), F32),
                shape((full, spans), BF16),
                shape((TAGS, spans), F32),
            ],
            (biaffine, act_got),
            flops=2 * labels * inner * full * spans,
        )
        score_got = exchange(score_parts, ("x", "z"))
        score_sum = jnp.sum(score_got, axis=0)
        scores = exchange(jnp.broadcast_to(score_sum[None], score_got.shape), ("x", "z"))

        grad_pay, outer, loss = call(
            lambda *refs: slope_body(nx, nz, inner, own, *refs),
            [
                shape((nx, full + inner, group), BF16),
                shape((labels * inner, spans), BF16),
                shape((1, spans), F32),
            ],
            (biaffine, left, right, all_tags, scores),
            scratch=(pltpu.VMEM((labels, spans), F32),),
            flops=4 * labels * inner * full * spans,
        )
        span_loss = lax.dynamic_slice_in_dim(loss, seq_index * own, own, 1)
        (flat,) = call(
            flat_body,
            [shape((labels * inner, full), BF16)],
            (outer, right),
            flops=2 * labels * inner * full * spans,
        )
        grad_biaffine = lax.psum(flat, ("y", "core")).reshape(labels, inner, full)

        grad_got = exchange(grad_pay, "x")
        (fold_pay,) = call(
            lambda *refs: fold_body(nx, nz, *refs),
            [shape((nz, rows, group), BF16)],
            (grad_got,),
        )
        fold_got = exchange(fold_pay, "z")
        (lowered,) = call(
            lambda *refs: lower_body(ny, nx, nz, inner, *refs),
            [shape((ny * CORES * nz, rows // ny, group), BF16)],
            (pre, grad_got, fold_got),
        )
        lowered_got = exchange(lowered, ("y", "core", "z"))
        (grad_parts,) = call(
            lambda *refs: weight_body(ny, nx, nz, inner, *refs),
            [shape((nx, depth, width), BF16)],
            (lowered_got, all_pieces),
            scratch=(pltpu.VMEM((width, ny * CORES * group), BF16),),
            flops=2 * full * nx * depth * group * CORES,
        )
        (grad_own,) = call(
            total_body, [shape((ny * CORES, depth, width), BF16)], (exchange(grad_parts, "x"),)
        )
        grad_start, grad_end = call(
            join_body,
            [shape((depth, full), BF16), shape((depth, full), BF16)],
            (exchange(grad_own, ("y", "core")),),
        )
        return span_loss, grad_start, grad_end, grad_biaffine

    return shards


def solution(mesh):
    ny, nz = mesh.shape["dp"] // CORES, mesh.shape["seq"] // COLUMNS
    fine = Mesh(mesh.devices.reshape(ny, CORES, COLUMNS, nz), ("y", "core", "x", "z"))
    dp, seq = ("y", "core"), ("x", "z")
    placed = (
        P(dp, seq, None),
        P(dp, seq),
        P(dp, seq),
        P(dp, seq),
        P(dp, seq),
        P(seq, None),
        P(seq, None),
        P(None, seq, None),
    )
    return jax.shard_map(
        build(ny, COLUMNS, nz),
        mesh=fine,
        in_specs=placed,
        out_specs=(P(dp, seq), P(seq, None), P(seq, None), P(None, seq, None)),
        check_vma=False,
    )
```

```python
import jax
import jax.numpy as jnp
from jax import lax
from jax.experimental import pallas as pl
from jax.experimental.pallas import tpu as pltpu
from jax.sharding import Mesh
from jax.sharding import PartitionSpec as P

CORES = 2
COLUMNS = 4
BF16 = jnp.bfloat16
F32 = jnp.float32


def exchange(parts, axes):
    return lax.all_to_all(parts, axes, split_axis=0, concat_axis=0, tiled=True)


def call(body, outs, args, scratch=(), smem=(), hbm=(), flops=0, room=16):
    moved = sum(a.size * a.dtype.itemsize for a in args)
    moved += sum(o.size * jnp.dtype(o.dtype).itemsize for o in outs)
    specs = [
        pl.BlockSpec(
            memory_space=pltpu.SMEM if i in smem else pltpu.HBM if i in hbm else pltpu.VMEM
        )
        for i in range(len(args))
    ]
    got = pl.pallas_call(
        body,
        out_shape=tuple(outs),
        in_specs=specs,
        out_specs=tuple(pl.BlockSpec(memory_space=pltpu.VMEM) for _ in outs),
        scratch_shapes=list(scratch),
        compiler_params=pltpu.CompilerParams(vmem_limit_bytes=room * 1024 * 1024),
        cost_estimate=pl.CostEstimate(flops=flops, bytes_accessed=moved, transcendentals=0),
    )(*args)
    return got


def dot(a, b, da, db):
    return lax.dot_general(a, b, (((da,), (db,)), ((), ())), preferred_element_type=F32)


def pick_body(
    nx, nz, seq_ref, start_hbm, end_hbm, states_hbm, out_ref, start_ref, end_ref, states_ref, sems
):
    tokens, width = states_ref.shape
    half = tokens // 2
    depth = width // (nx * nz)
    own = start_ref.shape[1]
    copies = [
        pltpu.make_async_copy(states_hbm, states_ref, sems.at[0]),
        pltpu.make_async_copy(start_hbm, start_ref, sems.at[1]),
        pltpu.make_async_copy(end_hbm, end_ref, sems.at[2]),
    ]
    for copy in copies:
        copy.start()
    for copy in copies[1:] + copies[:1]:
        copy.wait()
    states = states_ref[...]
    for side, ref in enumerate((start_ref, end_ref)):
        token = ref[...]
        inside = lax.rem(token, half)
        low = (token - inside) == seq_ref[0] * half
        picks = inside + jnp.where(low, 0, half)
        spot = lax.broadcasted_iota(jnp.int32, (tokens, own), 0)
        mask = jnp.where(spot == picks, 1.0, 0.0).astype(BF16)
        rows = dot(mask, states, 0, 0)
        for z in range(nz):
            cut = [rows[:, (x * nz + z) * depth : (x * nz + z + 1) * depth] for x in range(nx)]
            out_ref[side * nz + z] = jnp.concatenate(cut, axis=1).astype(BF16)


def project_body(nx, nz, inner, weight_ref, piece_ref, out_ref):
    full = weight_ref.shape[2]
    weight = weight_ref[...].reshape(-1, full)
    piece = piece_ref[...].reshape(-1, piece_ref.shape[2])
    pre = dot(weight, piece, 0, 1).astype(BF16)
    group = pre.shape[1] // CORES
    for c in range(CORES):
        for z in range(nz):
            for x in range(nx):
                at = (x * nz + z) * inner
                out_ref[c * nz + z, x * inner : (x + 1) * inner, :] = pre[
                    at : at + inner, c * group : (c + 1) * group
                ]


def act_body(nx, nz, got_ref, pre_ref, left_ref, right_ref):
    def total(side):
        sums = got_ref[side * nz].astype(F32)
        for z in range(1, nz):
            sums = sums + got_ref[side * nz + z].astype(F32)
        return sums

    pre_left, pre_right = total(0), total(1)
    pre_ref[0] = pre_left
    pre_ref[1] = pre_right
    left_ref[...] = jax.nn.gelu(pre_left).astype(BF16)
    block = jax.nn.gelu(pre_right).astype(BF16)
    for z in range(nz):
        right_ref[z] = block


def spread_body(nx, nz, inner, left_ref, got_ref, out_ref):
    full = nx * nz * inner
    for to in range(nx):
        for z in range(nz):
            for x in range(nx):
                at = (x * nz + z) * inner
                out_ref[to, at : at + inner, :] = got_ref[z, x * inner : (x + 1) * inner, :]
        out_ref[to, full : full + inner, :] = left_ref[to * inner : (to + 1) * inner, :]


def score_body(nx, nz, inner, weight_ref, got_ref, tags_ref, out_ref, left_ref, right_ref):
    labels, _, full = weight_ref.shape
    group = got_ref.shape[2]
    for x in range(nx):
        lanes = slice(x * group, (x + 1) * group)
        right_ref[:, lanes] = got_ref[x, :full, :]
        left_ref[:, lanes] = got_ref[x, full : full + inner, :].astype(F32)
    for i in range(nx * nz):
        if i % nz == labels // 8:
            out_ref[i] = tags_ref[i // nz]
        elif i % nz > labels // 8:
            out_ref[i] = jnp.zeros((8, group), F32)

    def step(lb, carry):
        weight = weight_ref[pl.ds(lb * 8, 8)].reshape(8 * inner, full)
        image = dot(weight, right_ref[...], 1, 0).reshape(8, inner, nx * group)
        total = jnp.sum(image * left_ref[...][None], axis=1)
        for x in range(nx):
            out_ref[x * nz + lb] = total[:, x * group : (x + 1) * group]
        return carry

    lax.fori_loop(0, labels // 8, step, 0)


def slope_body(
    nx, nz, inner, own, weight_ref, left_ref, right_ref, score_ref,
    out_ref, outer_ref, loss_ref, slope_ref,
):
    labels, _, full = weight_ref.shape
    group = score_ref.shape[2]
    spans = nx * group
    scores = jnp.concatenate(
        [
            jnp.concatenate([score_ref[x * nz + b] for x in range(nx)], axis=1)
            for b in range(labels // 8)
        ],
        axis=0,
    )
    tags = jnp.concatenate([score_ref[x * nz + labels // 8] for x in range(nx)], axis=1)
    gold, live = tags[0:1], tags[1:2]
    most = jnp.max(scores, axis=0, keepdims=True)
    log_total = most + jnp.log(jnp.sum(jnp.exp(scores - most), axis=0, keepdims=True))
    spot = lax.broadcasted_iota(jnp.int32, scores.shape, 0).astype(F32)
    onehot = jnp.where(spot == gold, 1.0, 0.0)
    picked = jnp.sum(scores * onehot, axis=0, keepdims=True)
    loss_ref[...] = live * (log_total - picked)
    slope = live * (jnp.exp(scores - log_total) - onehot) / own
    slope_ref[...] = slope.astype(BF16).astype(F32)

    def step(lb, left_sum):
        slope = slope_ref[pl.ds(lb * 8, 8), :]
        weight = weight_ref[pl.ds(lb * 8, 8)].reshape(8 * inner, full)
        image = dot(weight, right_ref[...], 1, 0).reshape(8, inner, spans)
        outer = (slope[:, None, :] * left_ref[...][None]).astype(BF16)
        outer_ref[pl.ds(lb * 8 * inner, 8 * inner), :] = outer.reshape(8 * inner, spans)
        return left_sum + jnp.sum(image * slope[:, None, :], axis=0)

    left_sum = lax.fori_loop(0, labels // 8, step, jnp.zeros((inner, spans), F32)).astype(BF16)
    weight = weight_ref[...].reshape(labels * inner, full)
    right_sum = dot(weight, outer_ref[...], 0, 0).astype(BF16)
    for to in range(nx):
        lanes = slice(to * group, (to + 1) * group)
        for z in range(nz):
            for x in range(nx):
                at = (x * nz + z) * inner
                spot = (z * nx + x) * inner
                out_ref[to, spot : spot + inner, :] = right_sum[at : at + inner, lanes]
        out_ref[to, full : full + inner, :] = left_sum[:, lanes]


def flat_body(outer_ref, right_ref, *outs):
    half = outs[0].shape[0]
    for i, out_ref in enumerate(outs):
        out_ref[...] = dot(outer_ref[i * half : (i + 1) * half], right_ref[...], 1, 1).astype(BF16)


def fold_body(nx, nz, got_ref, out_ref):
    _, rows, _ = out_ref.shape
    for z in range(nz):
        block = got_ref[0, z * rows : (z + 1) * rows, :].astype(F32)
        for x in range(1, nx):
            block = block + got_ref[x, z * rows : (z + 1) * rows, :].astype(F32)
        out_ref[z] = block.astype(BF16)


def lower_body(ny, nx, nz, inner, pre_ref, left_got, right_got, out_ref):
    full = nx * nz * inner
    grad_left = jnp.concatenate(
        [left_got[x, full : full + inner, :].astype(F32) for x in range(nx)], axis=0
    )
    grad_right = right_got[0].astype(F32)
    for z in range(1, nz):
        grad_right = grad_right + right_got[z].astype(F32)
    take = grad_left.shape[0] // ny
    for side, grad in enumerate((grad_left, grad_right)):
        _, back = jax.vjp(jax.nn.gelu, pre_ref[side])
        lowered = back(grad)[0].astype(BF16)
        for y in range(ny):
            for z in range(nz):
                out_ref[(y * CORES + side) * nz + z] = lowered[y * take : (y + 1) * take]


def weight_body(ny, nx, nz, inner, low_ref, piece_ref, out_ref, wide_ref):
    group = low_ref.shape[2]
    for s in range(ny * CORES):
        for z in range(nz):
            wide_ref[z * inner : (z + 1) * inner, s * group : (s + 1) * group] = low_ref[s * nz + z]
    piece = piece_ref[...].reshape(-1, piece_ref.shape[3])
    grad = dot(piece, wide_ref[...], 0, 1).astype(BF16)
    depth = out_ref.shape[1]
    for x in range(nx):
        out_ref[x] = grad[x * depth : (x + 1) * depth]


def total_body(got_ref, out_ref):
    total = got_ref[0].astype(F32)
    for x in range(1, got_ref.shape[0]):
        total = total + got_ref[x].astype(F32)
    total = total.astype(BF16)
    for i in range(out_ref.shape[0]):
        out_ref[i] = total


def join_body(got_ref, start_ref, end_ref):
    width = got_ref.shape[2]
    for y in range(got_ref.shape[0] // CORES):
        start_ref[:, y * width : (y + 1) * width] = got_ref[y * CORES]
        end_ref[:, y * width : (y + 1) * width] = got_ref[y * CORES + 1]


def build(ny, nx, nz):
    def shards(states, span_start, span_end, gold, live, start_proj, end_proj, biaffine):
        x_index, z_index = lax.axis_index("x"), lax.axis_index("z")
        seq_index = x_index * nz + z_index
        core = lax.axis_index("core")
        own = span_start.shape[1]
        labels, inner, full = biaffine.shape
        depth = start_proj.shape[0]
        group = own * nz
        spans = group * nx
        width = full // ny
        rows = nx * inner
        shape = jax.ShapeDtypeStruct

        side_proj = jnp.where(core == 0, start_proj, end_proj)
        weights = lax.all_gather(side_proj, "x", axis=0)

        (picked,) = call(
            lambda *refs: pick_body(nx, nz, *refs),
            [shape((CORES * nz, own, nx * depth), BF16)],
            (seq_index.reshape(1), span_start, span_end, states[0]),
            scratch=(
                pltpu.VMEM(span_start.shape, jnp.int32),
                pltpu.VMEM(span_end.shape, jnp.int32),
                pltpu.VMEM(states.shape[1:], BF16),
                pltpu.SemaphoreType.DMA((3,)),
            ),
            smem=(0,),
            hbm=(1, 2, 3),
        )
        pieces = exchange(picked, ("core", "z"))
        all_pieces = lax.all_gather(pieces, "y", axis=0)

        (pre_parts,) = call(
            lambda *refs: project_body(nx, nz, inner, *refs),
            [shape((CORES * nz, rows, group), BF16)],
            (weights, pieces),
            flops=2 * full * nx * depth * group * CORES,
        )
        pre_got = exchange(pre_parts, ("core", "z"))

        tags = jnp.concatenate([gold, live], axis=0).astype(F32)[None]
        tags = lax.dynamic_update_slice(
            jnp.zeros((nx, 8, group), F32), tags, (x_index, 0, z_index * own)
        )
        pre, left_own, right_pay = call(
            lambda *refs: act_body(nx, nz, *refs),
            [
                shape((2, rows, group), F32),
                shape((rows, group), BF16),
                shape((nz, rows, group), BF16),
            ],
            (pre_got,),
        )
        right_column = exchange(right_pay, "z")
        (act_pay,) = call(
            lambda *refs: spread_body(nx, nz, inner, *refs),
            [shape((nx, full + inner, group), BF16)],
            (left_own, right_column),
        )
        act_got = exchange(act_pay, "x")

        score_parts, left, right = call(
            lambda *refs: score_body(nx, nz, inner, *refs),
            [
                shape((nx * nz, 8, group), F32),
                shape((inner, spans), F32),
                shape((full, spans), BF16),
            ],
            (biaffine, act_got, tags),
            flops=2 * labels * inner * full * spans,
        )
        score_got = exchange(score_parts, ("x", "z"))
        score_sum = jnp.sum(score_got, axis=0)
        scores = exchange(jnp.broadcast_to(score_sum[None], score_got.shape), ("x", "z"))

        grad_pay, outer, loss = call(
            lambda *refs: slope_body(nx, nz, inner, own, *refs),
            [
                shape((nx, full + inner, group), BF16),
                shape((labels * inner, spans), BF16),
                shape((1, spans), F32),
            ],
            (biaffine, left, right, scores),
            scratch=(pltpu.VMEM((labels, spans), F32),),
            flops=4 * labels * inner * full * spans,
        )
        span_loss = lax.dynamic_slice_in_dim(loss, seq_index * own, own, 1)
        halves = call(
            flat_body,
            [shape((labels * inner // 2, full), BF16)] * 2,
            (outer, right),
            flops=2 * labels * inner * full * spans,
        )
        grad_got, _ = lax.optimization_barrier((exchange(grad_pay, "x"), halves))
        grad_biaffine = jnp.concatenate(
            [lax.psum(half, axes) for half, axes in zip(halves, (("y", "core"), ("core", "y")))],
            axis=0,
        ).reshape(labels, inner, full)
        (fold_pay,) = call(
            lambda *refs: fold_body(nx, nz, *refs),
            [shape((nz, rows, group), BF16)],
            (grad_got,),
        )
        fold_got = exchange(fold_pay, "z")
        (lowered,) = call(
            lambda *refs: lower_body(ny, nx, nz, inner, *refs),
            [shape((ny * CORES * nz, rows // ny, group), BF16)],
            (pre, grad_got, fold_got),
        )
        lowered_got = exchange(lowered, ("y", "core", "z"))
        (grad_parts,) = call(
            lambda *refs: weight_body(ny, nx, nz, inner, *refs),
            [shape((nx, depth, width), BF16)],
            (lowered_got, all_pieces),
            scratch=(pltpu.VMEM((width, ny * CORES * group), BF16),),
            flops=2 * full * nx * depth * group * CORES,
        )
        (grad_own,) = call(
            total_body, [shape((ny * CORES, depth, width), BF16)], (exchange(grad_parts, "x"),)
        )
        grad_start, grad_end = call(
            join_body,
            [shape((depth, full), BF16), shape((depth, full), BF16)],
            (exchange(grad_own, ("y", "core")),),
        )
        return span_loss, grad_start, grad_end, grad_biaffine

    return shards


def solution(mesh):
    ny, nz = mesh.shape["dp"] // CORES, mesh.shape["seq"] // COLUMNS
    fine = Mesh(mesh.devices.reshape(ny, CORES, COLUMNS, nz), ("y", "core", "x", "z"))
    dp, seq = ("y", "core"), ("x", "z")
    placed = (
        P(dp, seq, None),
        P(dp, seq),
        P(dp, seq),
        P(dp, seq),
        P(dp, seq),
        P(seq, None),
        P(seq, None),
        P(None, seq, None),
    )
    return jax.shard_map(
        build(ny, COLUMNS, nz),
        mesh=fine,
        in_specs=placed,
        out_specs=(P(dp, seq), P(seq, None), P(seq, None), P(None, seq, None)),
        check_vma=False,
    )
```

```python
import jax
import jax.numpy as jnp
from jax import lax
from jax.experimental import pallas as pl
from jax.experimental.pallas import tpu as pltpu
from jax.sharding import Mesh
from jax.sharding import PartitionSpec as P

CORES = 2
COLUMNS = 4
BF16 = jnp.bfloat16
F32 = jnp.float32


def exchange(parts, axes):
    return lax.all_to_all(parts, axes, split_axis=0, concat_axis=0, tiled=True)


def call(body, outs, args, scratch=(), smem=(), flops=0, room=16):
    moved = sum(a.size * a.dtype.itemsize for a in args)
    moved += sum(o.size * jnp.dtype(o.dtype).itemsize for o in outs)
    specs = [
        pl.BlockSpec(memory_space=pltpu.SMEM if i in smem else pltpu.VMEM)
        for i in range(len(args))
    ]
    got = pl.pallas_call(
        body,
        out_shape=tuple(outs),
        in_specs=specs,
        out_specs=tuple(pl.BlockSpec(memory_space=pltpu.VMEM) for _ in outs),
        scratch_shapes=list(scratch),
        compiler_params=pltpu.CompilerParams(vmem_limit_bytes=room * 1024 * 1024),
        cost_estimate=pl.CostEstimate(flops=flops, bytes_accessed=moved, transcendentals=0),
    )(*args)
    return got


def dot(a, b, da, db):
    return lax.dot_general(a, b, (((da,), (db,)), ((), ())), preferred_element_type=F32)


def pick_body(nx, nz, seq_ref, ends_ref, states_ref, out_ref):
    tokens, width = states_ref.shape
    half = tokens // 2
    depth = width // (nx * nz)
    own = ends_ref.shape[1]
    states = states_ref[...]
    for side in range(CORES):
        token = ends_ref[side : side + 1, :]
        inside = lax.rem(token, half)
        low = (token - inside) == seq_ref[0] * half
        picks = inside + jnp.where(low, 0, half)
        spot = lax.broadcasted_iota(jnp.int32, (tokens, own), 0)
        mask = jnp.where(spot == picks, 1.0, 0.0).astype(BF16)
        rows = dot(mask, states, 0, 0)
        for z in range(nz):
            cut = [rows[:, (x * nz + z) * depth : (x * nz + z + 1) * depth] for x in range(nx)]
            out_ref[side * nz + z] = jnp.concatenate(cut, axis=1).astype(BF16)


def project_body(nx, nz, inner, weight_ref, piece_ref, out_ref):
    full = weight_ref.shape[2]
    weight = weight_ref[...].reshape(-1, full)
    piece = piece_ref[...].reshape(-1, piece_ref.shape[2])
    pre = dot(weight, piece, 0, 1).astype(BF16)
    group = pre.shape[1] // CORES
    for c in range(CORES):
        for z in range(nz):
            for x in range(nx):
                at = (x * nz + z) * inner
                out_ref[c * nz + z, x * inner : (x + 1) * inner, :] = pre[
                    at : at + inner, c * group : (c + 1) * group
                ]


def act_body(nx, nz, got_ref, pre_ref, left_ref, right_ref):
    def total(side):
        sums = got_ref[side * nz].astype(F32)
        for z in range(1, nz):
            sums = sums + got_ref[side * nz + z].astype(F32)
        return sums

    pre_left, pre_right = total(0), total(1)
    pre_ref[0] = pre_left
    pre_ref[1] = pre_right
    left_ref[...] = jax.nn.gelu(pre_left).astype(BF16)
    block = jax.nn.gelu(pre_right).astype(BF16)
    for z in range(nz):
        right_ref[z] = block


def spread_body(nx, nz, inner, left_ref, got_ref, out_ref):
    full = nx * nz * inner
    for to in range(nx):
        for z in range(nz):
            for x in range(nx):
                at = (x * nz + z) * inner
                out_ref[to, at : at + inner, :] = got_ref[z, x * inner : (x + 1) * inner, :]
        out_ref[to, full : full + inner, :] = left_ref[to * inner : (to + 1) * inner, :]


def score_body(nx, nz, inner, weight_ref, got_ref, tags_ref, out_ref, left_ref, right_ref):
    labels, _, full = weight_ref.shape
    group = got_ref.shape[2]
    for x in range(nx):
        lanes = slice(x * group, (x + 1) * group)
        right_ref[:, lanes] = got_ref[x, :full, :]
        left_ref[:, lanes] = got_ref[x, full : full + inner, :].astype(F32)
    for i in range(nx * nz):
        if i % nz == labels // 8:
            out_ref[i] = tags_ref[i // nz]
        elif i % nz > labels // 8:
            out_ref[i] = jnp.zeros((8, group), F32)

    def step(lb, carry):
        weight = weight_ref[pl.ds(lb * 8, 8)].reshape(8 * inner, full)
        image = dot(weight, right_ref[...], 1, 0).reshape(8, inner, nx * group)
        total = jnp.sum(image * left_ref[...][None], axis=1)
        for x in range(nx):
            out_ref[x * nz + lb] = total[:, x * group : (x + 1) * group]
        return carry

    lax.fori_loop(0, labels // 8, step, 0)


def slope_body(nx, nz, inner, own, labels, left_ref, score_ref, outer_ref, loss_ref, slope_ref):
    spans = left_ref.shape[1]
    scores = jnp.concatenate(
        [
            jnp.concatenate([score_ref[x * nz + b] for x in range(nx)], axis=1)
            for b in range(labels // 8)
        ],
        axis=0,
    )
    tags = jnp.concatenate([score_ref[x * nz + labels // 8] for x in range(nx)], axis=1)
    gold, live = tags[0:1], tags[1:2]
    most = jnp.max(scores, axis=0, keepdims=True)
    log_total = most + jnp.log(jnp.sum(jnp.exp(scores - most), axis=0, keepdims=True))
    spot = lax.broadcasted_iota(jnp.int32, scores.shape, 0).astype(F32)
    onehot = jnp.where(spot == gold, 1.0, 0.0)
    picked = jnp.sum(scores * onehot, axis=0, keepdims=True)
    loss_ref[...] = live * (log_total - picked)
    slope = live * (jnp.exp(scores - log_total) - onehot) / own
    slope_ref[...] = slope.astype(BF16).astype(F32)

    def step(lb, carry):
        slope = slope_ref[pl.ds(lb * 8, 8), :]
        outer = (slope[:, None, :] * left_ref[...][None]).astype(BF16)
        outer_ref[pl.ds(lb * 8 * inner, 8 * inner), :] = outer.reshape(8 * inner, spans)
        return carry

    lax.fori_loop(0, labels // 8, step, 0)


def back_body(nx, nz, inner, weight_ref, right_ref, slope_ref, outer_ref, out_ref):
    labels, _, full = weight_ref.shape
    group = out_ref.shape[2]
    spans = nx * group

    def step(lb, left_sum):
        slope = slope_ref[pl.ds(lb * 8, 8), :]
        weight = weight_ref[pl.ds(lb * 8, 8)].reshape(8 * inner, full)
        image = dot(weight, right_ref[...], 1, 0).reshape(8, inner, spans)
        return left_sum + jnp.sum(image * slope[:, None, :], axis=0)

    left_sum = lax.fori_loop(0, labels // 8, step, jnp.zeros((inner, spans), F32)).astype(BF16)
    weight = weight_ref[...].reshape(labels * inner, full)
    right_sum = dot(weight, outer_ref[...], 0, 0).astype(BF16)
    for to in range(nx):
        lanes = slice(to * group, (to + 1) * group)
        for z in range(nz):
            for x in range(nx):
                at = (x * nz + z) * inner
                spot = (z * nx + x) * inner
                out_ref[to, spot : spot + inner, :] = right_sum[at : at + inner, lanes]
        out_ref[to, full : full + inner, :] = left_sum[:, lanes]


def flat_body(outer_ref, right_ref, out_ref):
    out_ref[...] = dot(outer_ref[...], right_ref[...], 1, 1)


def round_body(wide_ref, out_ref):
    out_ref[...] = wide_ref[...].astype(BF16)


def fold_body(nx, nz, got_ref, out_ref):
    _, rows, _ = out_ref.shape
    for z in range(nz):
        block = got_ref[0, z * rows : (z + 1) * rows, :].astype(F32)
        for x in range(1, nx):
            block = block + got_ref[x, z * rows : (z + 1) * rows, :].astype(F32)
        out_ref[z] = block.astype(BF16)


def lower_body(ny, nx, nz, inner, pre_ref, left_got, right_got, out_ref):
    full = nx * nz * inner
    grad_left = jnp.concatenate(
        [left_got[x, full : full + inner, :].astype(F32) for x in range(nx)], axis=0
    )
    grad_right = right_got[0].astype(F32)
    for z in range(1, nz):
        grad_right = grad_right + right_got[z].astype(F32)
    take = grad_left.shape[0] // ny
    for side, grad in enumerate((grad_left, grad_right)):
        _, back = jax.vjp(jax.nn.gelu, pre_ref[side])
        lowered = back(grad)[0].astype(BF16)
        for y in range(ny):
            for z in range(nz):
                out_ref[(y * CORES + side) * nz + z] = lowered[y * take : (y + 1) * take]


def weight_body(ny, nx, nz, inner, low_ref, piece_ref, out_ref, wide_ref):
    group = low_ref.shape[2]
    for s in range(ny * CORES):
        for z in range(nz):
            wide_ref[z * inner : (z + 1) * inner, s * group : (s + 1) * group] = low_ref[s * nz + z]
    piece = piece_ref[...].reshape(-1, piece_ref.shape[3])
    grad = dot(piece, wide_ref[...], 0, 1).astype(BF16)
    depth = out_ref.shape[1]
    for x in range(nx):
        out_ref[x] = grad[x * depth : (x + 1) * depth]


def total_body(got_ref, out_ref):
    total = got_ref[0].astype(F32)
    for x in range(1, got_ref.shape[0]):
        total = total + got_ref[x].astype(F32)
    total = total.astype(BF16)
    for i in range(out_ref.shape[0]):
        out_ref[i] = total


def join_body(got_ref, start_ref, end_ref):
    width = got_ref.shape[2]
    for y in range(got_ref.shape[0] // CORES):
        start_ref[:, y * width : (y + 1) * width] = got_ref[y * CORES]
        end_ref[:, y * width : (y + 1) * width] = got_ref[y * CORES + 1]


def build(ny, nx, nz):
    def shards(states, span_start, span_end, gold, live, start_proj, end_proj, biaffine):
        x_index, z_index = lax.axis_index("x"), lax.axis_index("z")
        seq_index = x_index * nz + z_index
        core = lax.axis_index("core")
        own = span_start.shape[1]
        labels, inner, full = biaffine.shape
        depth = start_proj.shape[0]
        group = own * nz
        spans = group * nx
        width = full // ny
        rows = nx * inner
        shape = jax.ShapeDtypeStruct

        side_proj = jnp.where(core == 0, start_proj, end_proj)
        weights = lax.all_gather(side_proj, "x", axis=0)

        (picked,) = call(
            lambda *refs: pick_body(nx, nz, *refs),
            [shape((CORES * nz, own, nx * depth), BF16)],
            (seq_index.reshape(1), jnp.concatenate([span_start, span_end], axis=0), states[0]),
            smem=(0,),
        )
        pieces = exchange(picked, ("core", "z"))
        all_pieces = lax.all_gather(pieces, "y", axis=0)

        (pre_parts,) = call(
            lambda *refs: project_body(nx, nz, inner, *refs),
            [shape((CORES * nz, rows, group), BF16)],
            (weights, pieces),
            flops=2 * full * nx * depth * group * CORES,
        )
        pre_got = exchange(pre_parts, ("core", "z"))

        tags = jnp.concatenate([gold, live], axis=0).astype(F32)[None]
        tags = lax.dynamic_update_slice(
            jnp.zeros((nx, 8, group), F32), tags, (x_index, 0, z_index * own)
        )
        pre, left_own, right_pay = call(
            lambda *refs: act_body(nx, nz, *refs),
            [
                shape((2, rows, group), F32),
                shape((rows, group), BF16),
                shape((nz, rows, group), BF16),
            ],
            (pre_got,),
        )
        right_column = exchange(right_pay, "z")
        (act_pay,) = call(
            lambda *refs: spread_body(nx, nz, inner, *refs),
            [shape((nx, full + inner, group), BF16)],
            (left_own, right_column),
        )
        act_got = exchange(act_pay, "x")

        score_parts, left, right = call(
            lambda *refs: score_body(nx, nz, inner, *refs),
            [
                shape((nx * nz, 8, group), F32),
                shape((inner, spans), F32),
                shape((full, spans), BF16),
            ],
            (biaffine, act_got, tags),
            flops=2 * labels * inner * full * spans,
        )
        score_got = exchange(score_parts, ("x", "z"))
        score_sum = jnp.sum(score_got, axis=0)
        scores = exchange(jnp.broadcast_to(score_sum[None], score_got.shape), ("x", "z"))

        outer, loss, slope = call(
            lambda *refs: slope_body(nx, nz, inner, own, labels, *refs),
            [
                shape((labels * inner, spans), BF16),
                shape((1, spans), F32),
                shape((labels, spans), F32),
            ],
            (left, scores),
        )
        span_loss = lax.dynamic_slice_in_dim(loss, seq_index * own, own, 1)
        (flat,) = call(
            flat_body,
            [shape((labels * inner, full), F32)],
            (outer, right),
            flops=2 * labels * inner * full * spans,
        )
        flat, slope = lax.optimization_barrier((flat, slope))
        (grad_pay,) = call(
            lambda *refs: back_body(nx, nz, inner, *refs),
            [shape((nx, full + inner, group), BF16)],
            (biaffine, right, slope, outer),
            flops=4 * labels * inner * full * spans,
        )
        grad_got = exchange(grad_pay, "x")
        (grad_biaffine,) = call(
            round_body,
            [shape((labels * inner, full), BF16)],
            (lax.psum(flat, ("y", "core")),),
            room=32,
        )
        grad_biaffine = grad_biaffine.reshape(labels, inner, full)
        (fold_pay,) = call(
            lambda *refs: fold_body(nx, nz, *refs),
            [shape((nz, rows, group), BF16)],
            (grad_got,),
        )
        fold_got = exchange(fold_pay, "z")
        (lowered,) = call(
            lambda *refs: lower_body(ny, nx, nz, inner, *refs),
            [shape((ny * CORES * nz, rows // ny, group), BF16)],
            (pre, grad_got, fold_got),
        )
        lowered_got = exchange(lowered, ("y", "core", "z"))
        (grad_parts,) = call(
            lambda *refs: weight_body(ny, nx, nz, inner, *refs),
            [shape((nx, depth, width), BF16)],
            (lowered_got, all_pieces),
            scratch=(pltpu.VMEM((width, ny * CORES * group), BF16),),
            flops=2 * full * nx * depth * group * CORES,
        )
        (grad_own,) = call(
            total_body, [shape((ny * CORES, depth, width), BF16)], (exchange(grad_parts, "x"),)
        )
        grad_start, grad_end = call(
            join_body,
            [shape((depth, full), BF16), shape((depth, full), BF16)],
            (exchange(grad_own, ("y", "core")),),
        )
        return span_loss, grad_start, grad_end, grad_biaffine

    return shards


def solution(mesh):
    ny, nz = mesh.shape["dp"] // CORES, mesh.shape["seq"] // COLUMNS
    fine = Mesh(mesh.devices.reshape(ny, CORES, COLUMNS, nz), ("y", "core", "x", "z"))
    dp, seq = ("y", "core"), ("x", "z")
    placed = (
        P(dp, seq, None),
        P(dp, seq),
        P(dp, seq),
        P(dp, seq),
        P(dp, seq),
        P(seq, None),
        P(seq, None),
        P(None, seq, None),
    )
    return jax.shard_map(
        build(ny, COLUMNS, nz),
        mesh=fine,
        in_specs=placed,
        out_specs=(P(dp, seq), P(seq, None), P(seq, None), P(None, seq, None)),
        check_vma=False,
    )
```

```python
import jax
import jax.numpy as jnp
from jax import lax
from jax.experimental import pallas as pl
from jax.experimental.pallas import tpu as pltpu
from jax.sharding import Mesh
from jax.sharding import PartitionSpec as P

CORES = 2
COLUMNS = 4
BF16 = jnp.bfloat16
F32 = jnp.float32


def exchange(parts, axes):
    return lax.all_to_all(parts, axes, split_axis=0, concat_axis=0, tiled=True)


def call(body, outs, args, scratch=(), smem=(), flops=0, room=16):
    moved = sum(a.size * a.dtype.itemsize for a in args)
    moved += sum(o.size * jnp.dtype(o.dtype).itemsize for o in outs)
    specs = [
        pl.BlockSpec(memory_space=pltpu.SMEM if i in smem else pltpu.VMEM)
        for i in range(len(args))
    ]
    got = pl.pallas_call(
        body,
        out_shape=tuple(outs),
        in_specs=specs,
        out_specs=tuple(pl.BlockSpec(memory_space=pltpu.VMEM) for _ in outs),
        scratch_shapes=list(scratch),
        compiler_params=pltpu.CompilerParams(vmem_limit_bytes=room * 1024 * 1024),
        cost_estimate=pl.CostEstimate(flops=flops, bytes_accessed=moved, transcendentals=0),
    )(*args)
    return got


def dot(a, b, da, db):
    return lax.dot_general(a, b, (((da,), (db,)), ((), ())), preferred_element_type=F32)


def pick_body(nx, nz, seq_ref, ends_ref, states_ref, out_ref):
    tokens, width = states_ref.shape
    half = tokens // 2
    depth = width // (nx * nz)
    own = ends_ref.shape[1]
    states = states_ref[...]
    for side in range(CORES):
        token = ends_ref[side : side + 1, :]
        inside = lax.rem(token, half)
        low = (token - inside) == seq_ref[0] * half
        picks = inside + jnp.where(low, 0, half)
        spot = lax.broadcasted_iota(jnp.int32, (tokens, own), 0)
        mask = jnp.where(spot == picks, 1.0, 0.0).astype(BF16)
        rows = dot(mask, states, 0, 0)
        for z in range(nz):
            cut = [rows[:, (x * nz + z) * depth : (x * nz + z + 1) * depth] for x in range(nx)]
            out_ref[side * nz + z] = jnp.concatenate(cut, axis=1).astype(BF16)


def project_body(nx, nz, inner, weight_ref, piece_ref, out_ref):
    full = weight_ref.shape[2]
    weight = weight_ref[...].reshape(-1, full)
    piece = piece_ref[...].reshape(-1, piece_ref.shape[2])
    pre = dot(weight, piece, 0, 1).astype(BF16)
    group = pre.shape[1] // CORES
    for c in range(CORES):
        for z in range(nz):
            for x in range(nx):
                at = (x * nz + z) * inner
                out_ref[c * nz + z, x * inner : (x + 1) * inner, :] = pre[
                    at : at + inner, c * group : (c + 1) * group
                ]


def act_body(nx, nz, got_ref, pre_ref, left_ref, right_ref):
    def total(side):
        sums = got_ref[side * nz].astype(F32)
        for z in range(1, nz):
            sums = sums + got_ref[side * nz + z].astype(F32)
        return sums

    pre_left, pre_right = total(0), total(1)
    pre_ref[0] = pre_left
    pre_ref[1] = pre_right
    left_ref[...] = jax.nn.gelu(pre_left).astype(BF16)
    block = jax.nn.gelu(pre_right).astype(BF16)
    for z in range(nz):
        right_ref[z] = block


def spread_body(nx, nz, inner, left_ref, got_ref, out_ref):
    full = nx * nz * inner
    for to in range(nx):
        for z in range(nz):
            for x in range(nx):
                at = (x * nz + z) * inner
                out_ref[to, at : at + inner, :] = got_ref[z, x * inner : (x + 1) * inner, :]
        out_ref[to, full : full + inner, :] = left_ref[to * inner : (to + 1) * inner, :]


def score_body(nx, nz, inner, weight_ref, got_ref, tags_ref, out_ref, left_ref, right_ref):
    labels, _, full = weight_ref.shape
    group = got_ref.shape[2]
    for x in range(nx):
        lanes = slice(x * group, (x + 1) * group)
        right_ref[:, lanes] = got_ref[x, :full, :]
        left_ref[:, lanes] = got_ref[x, full : full + inner, :].astype(F32)
    for i in range(nx * nz):
        if i % nz == labels // 8:
            out_ref[i] = tags_ref[i // nz]
        elif i % nz > labels // 8:
            out_ref[i] = jnp.zeros((8, group), F32)

    def step(lb, carry):
        weight = weight_ref[pl.ds(lb * 8, 8)].reshape(8 * inner, full)
        image = dot(weight, right_ref[...], 1, 0).reshape(8, inner, nx * group)
        total = jnp.sum(image * left_ref[...][None], axis=1)
        for x in range(nx):
            out_ref[x * nz + lb] = total[:, x * group : (x + 1) * group]
        return carry

    lax.fori_loop(0, labels // 8, step, 0)


def slope_body(nx, nz, inner, own, labels, left_ref, score_ref, outer_ref, loss_ref, slope_ref):
    spans = left_ref.shape[1]
    scores = jnp.concatenate(
        [
            jnp.concatenate([score_ref[x * nz + b] for x in range(nx)], axis=1)
            for b in range(labels // 8)
        ],
        axis=0,
    )
    tags = jnp.concatenate([score_ref[x * nz + labels // 8] for x in range(nx)], axis=1)
    gold, live = tags[0:1], tags[1:2]
    most = jnp.max(scores, axis=0, keepdims=True)
    log_total = most + jnp.log(jnp.sum(jnp.exp(scores - most), axis=0, keepdims=True))
    spot = lax.broadcasted_iota(jnp.int32, scores.shape, 0).astype(F32)
    onehot = jnp.where(spot == gold, 1.0, 0.0)
    picked = jnp.sum(scores * onehot, axis=0, keepdims=True)
    loss_ref[...] = live * (log_total - picked)
    slope = live * (jnp.exp(scores - log_total) - onehot) / own
    slope_ref[...] = slope.astype(BF16).astype(F32)

    def step(lb, carry):
        slope = slope_ref[pl.ds(lb * 8, 8), :]
        outer = (slope[:, None, :] * left_ref[...][None]).astype(BF16)
        outer_ref[pl.ds(lb * 8 * inner, 8 * inner), :] = outer.reshape(8 * inner, spans)
        return carry

    lax.fori_loop(0, labels // 8, step, 0)


def back_body(nx, nz, inner, weight_ref, right_ref, slope_ref, outer_ref, out_ref):
    labels, _, full = weight_ref.shape
    group = out_ref.shape[2]
    spans = nx * group

    def step(lb, left_sum):
        slope = slope_ref[pl.ds(lb * 8, 8), :]
        weight = weight_ref[pl.ds(lb * 8, 8)].reshape(8 * inner, full)
        image = dot(weight, right_ref[...], 1, 0).reshape(8, inner, spans)
        return left_sum + jnp.sum(image * slope[:, None, :], axis=0)

    left_sum = lax.fori_loop(0, labels // 8, step, jnp.zeros((inner, spans), F32)).astype(BF16)
    weight = weight_ref[...].reshape(labels * inner, full)
    right_sum = dot(weight, outer_ref[...], 0, 0).astype(BF16)
    for to in range(nx):
        lanes = slice(to * group, (to + 1) * group)
        for z in range(nz):
            for x in range(nx):
                at = (x * nz + z) * inner
                rows = slice(x * inner, (x + 1) * inner)
                out_ref[to * nz + z, rows, :] = right_sum[at : at + inner, lanes]
            out_ref[to * nz + z, nx * inner : (nx + 1) * inner, :] = left_sum[:, lanes]


def flat_body(outer_ref, right_ref, *outs):
    take = outs[0].shape[0]
    for i, out_ref in enumerate(outs):
        out_ref[...] = dot(outer_ref[i * take : (i + 1) * take], right_ref[...], 1, 1).astype(BF16)


def lower_body(ny, nx, nz, inner, z_ref, pre_ref, got_ref, out_ref):
    rows = nx * inner
    grad_left = jnp.concatenate(
        [got_ref[x * nz + z_ref[0], rows : rows + inner, :].astype(F32) for x in range(nx)],
        axis=0,
    )
    grad_right = got_ref[0, :rows, :].astype(F32)
    for i in range(1, nx * nz):
        grad_right = grad_right + got_ref[i, :rows, :].astype(F32)
    take = grad_left.shape[0] // ny
    for side, grad in enumerate((grad_left, grad_right)):
        _, back = jax.vjp(jax.nn.gelu, pre_ref[side])
        lowered = back(grad)[0].astype(BF16)
        for y in range(ny):
            for z in range(nz):
                out_ref[(y * CORES + side) * nz + z] = lowered[y * take : (y + 1) * take]


def weight_body(ny, nx, nz, inner, low_ref, piece_ref, out_ref, wide_ref):
    group = low_ref.shape[2]
    for s in range(ny * CORES):
        for z in range(nz):
            wide_ref[z * inner : (z + 1) * inner, s * group : (s + 1) * group] = low_ref[s * nz + z]
    piece = piece_ref[...].reshape(-1, piece_ref.shape[3])
    grad = dot(piece, wide_ref[...], 0, 1).astype(BF16)
    depth = out_ref.shape[1]
    for x in range(nx):
        out_ref[x] = grad[x * depth : (x + 1) * depth]


def total_body(got_ref, out_ref):
    total = got_ref[0].astype(F32)
    for x in range(1, got_ref.shape[0]):
        total = total + got_ref[x].astype(F32)
    total = total.astype(BF16)
    for i in range(out_ref.shape[0]):
        out_ref[i] = total


def join_body(got_ref, start_ref, end_ref):
    width = got_ref.shape[2]
    for y in range(got_ref.shape[0] // CORES):
        start_ref[:, y * width : (y + 1) * width] = got_ref[y * CORES]
        end_ref[:, y * width : (y + 1) * width] = got_ref[y * CORES + 1]


def build(ny, nx, nz):
    def shards(states, span_start, span_end, gold, live, start_proj, end_proj, biaffine):
        x_index, z_index = lax.axis_index("x"), lax.axis_index("z")
        seq_index = x_index * nz + z_index
        core = lax.axis_index("core")
        own = span_start.shape[1]
        labels, inner, full = biaffine.shape
        depth = start_proj.shape[0]
        group = own * nz
        spans = group * nx
        width = full // ny
        rows = nx * inner
        shape = jax.ShapeDtypeStruct

        side_proj = jnp.where(core == 0, start_proj, end_proj)
        weights = lax.all_gather(side_proj, "x", axis=0)

        (picked,) = call(
            lambda *refs: pick_body(nx, nz, *refs),
            [shape((CORES * nz, own, nx * depth), BF16)],
            (seq_index.reshape(1), jnp.concatenate([span_start, span_end], axis=0), states[0]),
            smem=(0,),
        )
        pieces = exchange(picked, ("core", "z"))
        all_pieces = lax.all_gather(pieces, "y", axis=0)

        (pre_parts,) = call(
            lambda *refs: project_body(nx, nz, inner, *refs),
            [shape((CORES * nz, rows, group), BF16)],
            (weights, pieces),
            flops=2 * full * nx * depth * group * CORES,
        )
        pre_got = exchange(pre_parts, ("core", "z"))

        tags = jnp.concatenate([gold, live], axis=0).astype(F32)[None]
        tags = lax.dynamic_update_slice(
            jnp.zeros((nx, 8, group), F32), tags, (x_index, 0, z_index * own)
        )
        pre, left_own, right_pay = call(
            lambda *refs: act_body(nx, nz, *refs),
            [
                shape((2, rows, group), F32),
                shape((rows, group), BF16),
                shape((nz, rows, group), BF16),
            ],
            (pre_got,),
        )
        right_column = exchange(right_pay, "z")
        (act_pay,) = call(
            lambda *refs: spread_body(nx, nz, inner, *refs),
            [shape((nx, full + inner, group), BF16)],
            (left_own, right_column),
        )
        act_got = exchange(act_pay, "x")

        score_parts, left, right = call(
            lambda *refs: score_body(nx, nz, inner, *refs),
            [
                shape((nx * nz, 8, group), F32),
                shape((inner, spans), F32),
                shape((full, spans), BF16),
            ],
            (biaffine, act_got, tags),
            flops=2 * labels * inner * full * spans,
        )
        score_got = exchange(score_parts, ("x", "z"))
        score_sum = jnp.sum(score_got, axis=0)
        scores = exchange(jnp.broadcast_to(score_sum[None], score_got.shape), ("x", "z"))

        outer, loss, slope = call(
            lambda *refs: slope_body(nx, nz, inner, own, labels, *refs),
            [
                shape((labels * inner, spans), BF16),
                shape((1, spans), F32),
                shape((labels, spans), F32),
            ],
            (left, scores),
        )
        span_loss = lax.dynamic_slice_in_dim(loss, seq_index * own, own, 1)
        flat = call(
            flat_body,
            [shape((labels * inner // 2, full), BF16)] * 2,
            (outer, right),
            flops=2 * labels * inner * full * spans,
        )
        flat, slope = lax.optimization_barrier((flat, slope))
        (grad_pay,) = call(
            lambda *refs: back_body(nx, nz, inner, *refs),
            [shape((nx * nz, rows + inner, group), BF16)],
            (biaffine, right, slope, outer),
            flops=4 * labels * inner * full * spans,
        )
        grad_got = exchange(grad_pay, ("x", "z"))
        grad_biaffine = jnp.concatenate(lax.psum(tuple(flat), ("y", "core")), axis=0).reshape(labels, inner, full)
        (lowered,) = call(
            lambda *refs: lower_body(ny, nx, nz, inner, *refs),
            [shape((ny * CORES * nz, rows // ny, group), BF16)],
            (z_index.reshape(1), pre, grad_got),
            smem=(0,),
        )
        lowered_got = exchange(lowered, ("y", "core", "z"))
        (grad_parts,) = call(
            lambda *refs: weight_body(ny, nx, nz, inner, *refs),
            [shape((nx, depth, width), BF16)],
            (lowered_got, all_pieces),
            scratch=(pltpu.VMEM((width, ny * CORES * group), BF16),),
            flops=2 * full * nx * depth * group * CORES,
        )
        (grad_own,) = call(
            total_body, [shape((ny * CORES, depth, width), BF16)], (exchange(grad_parts, "x"),)
        )
        grad_start, grad_end = call(
            join_body,
            [shape((depth, full), BF16), shape((depth, full), BF16)],
            (exchange(grad_own, ("y", "core")),),
        )
        return span_loss, grad_start, grad_end, grad_biaffine

    return shards


def solution(mesh):
    ny, nz = mesh.shape["dp"] // CORES, mesh.shape["seq"] // COLUMNS
    fine = Mesh(mesh.devices.reshape(ny, CORES, COLUMNS, nz), ("y", "core", "x", "z"))
    dp, seq = ("y", "core"), ("x", "z")
    placed = (
        P(dp, seq, None),
        P(dp, seq),
        P(dp, seq),
        P(dp, seq),
        P(dp, seq),
        P(seq, None),
        P(seq, None),
        P(None, seq, None),
    )
    return jax.shard_map(
        build(ny, COLUMNS, nz),
        mesh=fine,
        in_specs=placed,
        out_specs=(P(dp, seq), P(seq, None), P(seq, None), P(None, seq, None)),
        check_vma=False,
    )
```

```python
import jax
import jax.numpy as jnp
from jax import lax
from jax.experimental import pallas as pl
from jax.experimental.pallas import tpu as pltpu
from jax.sharding import Mesh
from jax.sharding import PartitionSpec as P

CORES = 2
COLUMNS = 4
BF16 = jnp.bfloat16
F32 = jnp.float32


def exchange(parts, axes):
    return lax.all_to_all(parts, axes, split_axis=0, concat_axis=0, tiled=True)


def call(body, outs, args, scratch=(), smem=(), flops=0, room=16):
    moved = sum(a.size * a.dtype.itemsize for a in args)
    moved += sum(o.size * jnp.dtype(o.dtype).itemsize for o in outs)
    specs = [
        pl.BlockSpec(memory_space=pltpu.SMEM if i in smem else pltpu.VMEM)
        for i in range(len(args))
    ]
    got = pl.pallas_call(
        body,
        out_shape=tuple(outs),
        in_specs=specs,
        out_specs=tuple(pl.BlockSpec(memory_space=pltpu.VMEM) for _ in outs),
        scratch_shapes=list(scratch),
        compiler_params=pltpu.CompilerParams(vmem_limit_bytes=room * 1024 * 1024),
        cost_estimate=pl.CostEstimate(flops=flops, bytes_accessed=moved, transcendentals=0),
    )(*args)
    return got


def dot(a, b, da, db):
    return lax.dot_general(a, b, (((da,), (db,)), ((), ())), preferred_element_type=F32)


def pick_body(nx, nz, seq_ref, ends_ref, states_ref, out_ref):
    tokens, width = states_ref.shape
    half = tokens // 2
    depth = width // (nx * nz)
    own = ends_ref.shape[1]
    states = states_ref[...]
    for side in range(CORES):
        token = ends_ref[side : side + 1, :]
        inside = lax.rem(token, half)
        low = (token - inside) == seq_ref[0] * half
        picks = inside + jnp.where(low, 0, half)
        spot = lax.broadcasted_iota(jnp.int32, (tokens, own), 0)
        mask = jnp.where(spot == picks, 1.0, 0.0).astype(BF16)
        rows = dot(mask, states, 0, 0)
        for z in range(nz):
            cut = [rows[:, (x * nz + z) * depth : (x * nz + z + 1) * depth] for x in range(nx)]
            out_ref[side * nz + z] = jnp.concatenate(cut, axis=1).astype(BF16)


def project_body(nx, nz, inner, weight_ref, piece_ref, out_ref):
    full = weight_ref.shape[2]
    weight = weight_ref[...].reshape(-1, full)
    piece = piece_ref[...].reshape(-1, piece_ref.shape[2])
    pre = dot(weight, piece, 0, 1).astype(BF16)
    group = pre.shape[1] // CORES
    for c in range(CORES):
        for z in range(nz):
            for x in range(nx):
                at = (x * nz + z) * inner
                out_ref[c * nz + z, x * inner : (x + 1) * inner, :] = pre[
                    at : at + inner, c * group : (c + 1) * group
                ]


def act_body(nx, nz, got_ref, pre_ref, left_ref, right_ref):
    def total(side):
        sums = got_ref[side * nz].astype(F32)
        for z in range(1, nz):
            sums = sums + got_ref[side * nz + z].astype(F32)
        return sums

    pre_left, pre_right = total(0), total(1)
    pre_ref[0] = pre_left
    pre_ref[1] = pre_right
    left_ref[...] = jax.nn.gelu(pre_left).astype(BF16)
    block = jax.nn.gelu(pre_right).astype(BF16)
    for z in range(nz):
        right_ref[z] = block


def spread_body(nx, nz, inner, left_ref, got_ref, out_ref):
    full = nx * nz * inner
    for to in range(nx):
        for z in range(nz):
            for x in range(nx):
                at = (x * nz + z) * inner
                out_ref[to, at : at + inner, :] = got_ref[z, x * inner : (x + 1) * inner, :]
        out_ref[to, full : full + inner, :] = left_ref[to * inner : (to + 1) * inner, :]


def score_body(nx, nz, inner, weight_ref, got_ref, tags_ref, out_ref, left_ref, right_ref):
    labels, _, full = weight_ref.shape
    group = got_ref.shape[2]
    for x in range(nx):
        lanes = slice(x * group, (x + 1) * group)
        right_ref[:, lanes] = got_ref[x, :full, :]
        left_ref[:, lanes] = got_ref[x, full : full + inner, :].astype(F32)
    for i in range(nx * nz):
        if i % nz == labels // 8:
            out_ref[i] = tags_ref[i // nz]
        elif i % nz > labels // 8:
            out_ref[i] = jnp.zeros((8, group), F32)

    def step(lb, carry):
        weight = weight_ref[pl.ds(lb * 8, 8)].reshape(8 * inner, full)
        image = dot(weight, right_ref[...], 1, 0).reshape(8, inner, nx * group)
        total = jnp.sum(image * left_ref[...][None], axis=1)
        for x in range(nx):
            out_ref[x * nz + lb] = total[:, x * group : (x + 1) * group]
        return carry

    lax.fori_loop(0, labels // 8, step, 0)


def slope_body(nx, nz, inner, own, labels, left_ref, score_ref, outer_ref, loss_ref, slope_ref):
    spans = left_ref.shape[1]
    scores = jnp.concatenate(
        [
            jnp.concatenate([score_ref[x * nz + b] for x in range(nx)], axis=1)
            for b in range(labels // 8)
        ],
        axis=0,
    )
    tags = jnp.concatenate([score_ref[x * nz + labels // 8] for x in range(nx)], axis=1)
    gold, live = tags[0:1], tags[1:2]
    most = jnp.max(scores, axis=0, keepdims=True)
    log_total = most + jnp.log(jnp.sum(jnp.exp(scores - most), axis=0, keepdims=True))
    spot = lax.broadcasted_iota(jnp.int32, scores.shape, 0).astype(F32)
    onehot = jnp.where(spot == gold, 1.0, 0.0)
    picked = jnp.sum(scores * onehot, axis=0, keepdims=True)
    loss_ref[...] = live * (log_total - picked)
    slope = live * (jnp.exp(scores - log_total) - onehot) / own
    slope_ref[...] = slope.astype(BF16).astype(F32)

    def step(lb, carry):
        slope = slope_ref[pl.ds(lb * 8, 8), :]
        outer = (slope[:, None, :] * left_ref[...][None]).astype(BF16)
        outer_ref[pl.ds(lb * 8 * inner, 8 * inner), :] = outer.reshape(8 * inner, spans)
        return carry

    lax.fori_loop(0, labels // 8, step, 0)


def back_body(nx, nz, inner, weight_ref, right_ref, slope_ref, outer_ref, out_ref):
    labels, _, full = weight_ref.shape
    group = out_ref.shape[2]
    spans = nx * group

    def step(lb, left_sum):
        slope = slope_ref[pl.ds(lb * 8, 8), :]
        weight = weight_ref[pl.ds(lb * 8, 8)].reshape(8 * inner, full)
        image = dot(weight, right_ref[...], 1, 0).reshape(8, inner, spans)
        return left_sum + jnp.sum(image * slope[:, None, :], axis=0)

    left_sum = lax.fori_loop(0, labels // 8, step, jnp.zeros((inner, spans), F32)).astype(BF16)
    weight = weight_ref[...].reshape(labels * inner, full)
    right_sum = dot(weight, outer_ref[...], 0, 0).astype(BF16)
    for to in range(nx):
        lanes = slice(to * group, (to + 1) * group)
        for z in range(nz):
            for x in range(nx):
                at = (x * nz + z) * inner
                rows = slice(x * inner, (x + 1) * inner)
                out_ref[to * nz + z, rows, :] = right_sum[at : at + inner, lanes]
            out_ref[to * nz + z, nx * inner : (nx + 1) * inner, :] = left_sum[:, lanes]


def flat_body(outer_ref, right_ref, *outs):
    take = outs[0].shape[0]
    for i, out_ref in enumerate(outs):
        out_ref[...] = dot(outer_ref[i * take : (i + 1) * take], right_ref[...], 1, 1).astype(BF16)


def lower_body(ny, nx, nz, inner, z_ref, pre_ref, got_ref, out_ref):
    rows = nx * inner
    grad_left = jnp.concatenate(
        [got_ref[x * nz + z_ref[0], rows : rows + inner, :].astype(F32) for x in range(nx)],
        axis=0,
    )
    grad_right = got_ref[0, :rows, :].astype(F32)
    for i in range(1, nx * nz):
        grad_right = grad_right + got_ref[i, :rows, :].astype(F32)
    take = grad_left.shape[0] // ny
    for side, grad in enumerate((grad_left, grad_right)):
        _, back = jax.vjp(jax.nn.gelu, pre_ref[side])
        lowered = back(grad)[0].astype(BF16)
        for y in range(ny):
            for z in range(nz):
                out_ref[(y * CORES + side) * nz + z] = lowered[y * take : (y + 1) * take]


def weight_body(ny, nx, nz, inner, low_ref, piece_ref, out_ref, wide_ref):
    group = low_ref.shape[2]
    for s in range(ny * CORES):
        for z in range(nz):
            wide_ref[z * inner : (z + 1) * inner, s * group : (s + 1) * group] = low_ref[s * nz + z]
    piece = piece_ref[...].reshape(-1, piece_ref.shape[3])
    grad = dot(piece, wide_ref[...], 0, 1).astype(BF16)
    depth = out_ref.shape[1]
    for x in range(nx):
        out_ref[x] = grad[x * depth : (x + 1) * depth]


def total_body(got_ref, out_ref):
    total = got_ref[0].astype(F32)
    for x in range(1, got_ref.shape[0]):
        total = total + got_ref[x].astype(F32)
    total = total.astype(BF16)
    for i in range(out_ref.shape[0]):
        out_ref[i] = total


def join_body(got_ref, start_ref, end_ref):
    width = got_ref.shape[2]
    for y in range(got_ref.shape[0] // CORES):
        start_ref[:, y * width : (y + 1) * width] = got_ref[y * CORES]
        end_ref[:, y * width : (y + 1) * width] = got_ref[y * CORES + 1]


def build(ny, nx, nz):
    def shards(states, span_start, span_end, gold, live, start_proj, end_proj, biaffine):
        x_index, z_index = lax.axis_index("x"), lax.axis_index("z")
        seq_index = x_index * nz + z_index
        core = lax.axis_index("core")
        own = span_start.shape[1]
        labels, inner, full = biaffine.shape
        depth = start_proj.shape[0]
        group = own * nz
        spans = group * nx
        width = full // ny
        rows = nx * inner
        shape = jax.ShapeDtypeStruct

        side_proj = jnp.where(core == 0, start_proj, end_proj)
        weights = lax.all_gather(side_proj, "x", axis=0)

        (picked,) = call(
            lambda *refs: pick_body(nx, nz, *refs),
            [shape((CORES * nz, own, nx * depth), BF16)],
            (seq_index.reshape(1), jnp.concatenate([span_start, span_end], axis=0), states[0]),
            smem=(0,),
        )
        pieces = exchange(picked, ("core", "z"))
        all_pieces = lax.all_gather(pieces, "y", axis=0)

        (pre_parts,) = call(
            lambda *refs: project_body(nx, nz, inner, *refs),
            [shape((CORES * nz, rows, group), BF16)],
            (weights, pieces),
            flops=2 * full * nx * depth * group * CORES,
        )
        pre_got = exchange(pre_parts, ("core", "z"))

        tags = jnp.concatenate([gold, live], axis=0).astype(F32)[None]
        tags = lax.dynamic_update_slice(
            jnp.zeros((nx, 8, group), F32), tags, (x_index, 0, z_index * own)
        )
        pre, left_own, right_pay = call(
            lambda *refs: act_body(nx, nz, *refs),
            [
                shape((2, rows, group), F32),
                shape((rows, group), BF16),
                shape((nz, rows, group), BF16),
            ],
            (pre_got,),
        )
        right_column = exchange(right_pay, "z")
        (act_pay,) = call(
            lambda *refs: spread_body(nx, nz, inner, *refs),
            [shape((nx, full + inner, group), BF16)],
            (left_own, right_column),
        )
        act_got = exchange(act_pay, "x")

        score_parts, left, right = call(
            lambda *refs: score_body(nx, nz, inner, *refs),
            [
                shape((nx * nz, 8, group), F32),
                shape((inner, spans), F32),
                shape((full, spans), BF16),
            ],
            (biaffine, act_got, tags),
            flops=2 * labels * inner * full * spans,
        )
        score_got = exchange(score_parts, ("x", "z"))
        score_sum = jnp.sum(score_got, axis=0)
        scores = exchange(jnp.broadcast_to(score_sum[None], score_got.shape), ("x", "z"))

        scores, all_pieces = lax.optimization_barrier((scores, all_pieces))
        outer, loss, slope = call(
            lambda *refs: slope_body(nx, nz, inner, own, labels, *refs),
            [
                shape((labels * inner, spans), BF16),
                shape((1, spans), F32),
                shape((labels, spans), F32),
            ],
            (left, scores),
        )
        span_loss = lax.dynamic_slice_in_dim(loss, seq_index * own, own, 1)
        flat = call(
            flat_body,
            [shape((labels * inner // 2, full), BF16)] * 2,
            (outer, right),
            flops=2 * labels * inner * full * spans,
        )
        flat, slope = lax.optimization_barrier((flat, slope))
        (grad_pay,) = call(
            lambda *refs: back_body(nx, nz, inner, *refs),
            [shape((nx * nz, rows + inner, group), BF16)],
            (biaffine, right, slope, outer),
            flops=4 * labels * inner * full * spans,
        )
        grad_got = exchange(grad_pay, ("x", "z"))
        grad_biaffine = jnp.concatenate(lax.psum(tuple(flat), ("y", "core")), axis=0).reshape(labels, inner, full)
        (lowered,) = call(
            lambda *refs: lower_body(ny, nx, nz, inner, *refs),
            [shape((ny * CORES * nz, rows // ny, group), BF16)],
            (z_index.reshape(1), pre, grad_got),
            smem=(0,),
        )
        lowered_got = exchange(lowered, ("y", "core", "z"))
        (grad_parts,) = call(
            lambda *refs: weight_body(ny, nx, nz, inner, *refs),
            [shape((nx, depth, width), BF16)],
            (lowered_got, all_pieces),
            scratch=(pltpu.VMEM((width, ny * CORES * group), BF16),),
            flops=2 * full * nx * depth * group * CORES,
        )
        (grad_own,) = call(
            total_body, [shape((ny * CORES, depth, width), BF16)], (exchange(grad_parts, "x"),)
        )
        grad_start, grad_end = call(
            join_body,
            [shape((depth, full), BF16), shape((depth, full), BF16)],
            (exchange(grad_own, ("y", "core")),),
        )
        return span_loss, grad_start, grad_end, grad_biaffine

    return shards


def solution(mesh):
    ny, nz = mesh.shape["dp"] // CORES, mesh.shape["seq"] // COLUMNS
    fine = Mesh(mesh.devices.reshape(ny, CORES, COLUMNS, nz), ("y", "core", "x", "z"))
    dp, seq = ("y", "core"), ("x", "z")
    placed = (
        P(dp, seq, None),
        P(dp, seq),
        P(dp, seq),
        P(dp, seq),
        P(dp, seq),
        P(seq, None),
        P(seq, None),
        P(None, seq, None),
    )
    return jax.shard_map(
        build(ny, COLUMNS, nz),
        mesh=fine,
        in_specs=placed,
        out_specs=(P(dp, seq), P(seq, None), P(seq, None), P(None, seq, None)),
        check_vma=False,
    )
```
